32 devices in a mesh: role: 2 (over y), dp: 4 (over z), tp: 4 (over x, core).
Axes of the slice: x: 2, y: 2, z: 4, core: 2. Of those that a mesh axis runs over, the one named last changes fastest.
Arguments:
- hidden: bfloat16 [2, 512, 8192], P('role', 'dp'), may hold values from -6 to 6
- out_grad: bfloat16 [512, 1024], P('dp', 'tp'), may hold values from -6 to 6
- master: float32 [8192, 1024], P('dp', 'tp'), may hold values from -0.0625 to 0.0625
- moment1: float32 [8192, 1024], P('dp', 'tp'), may hold values from -18 to 18
- moment2: float32 [8192, 1024], P('dp', 'tp'), may hold values from 50 to 500
- queries: bfloat16 [8, 64, 8192], P(None, 'dp', 'tp'), may hold values from -160 to 160
- new_keys: bfloat16 [8, 64, 1024], P(None, 'dp', 'tp'), may hold values from -6 to 6
- k_cache: bfloat16 [64, 256, 1024], P('dp', None, 'tp'), may hold values from -6 to 6
- v_cache: bfloat16 [64, 256, 1024], P('dp', None, 'tp'), may hold values from -6 to 6
- cache_len: int32 [64], P('dp'), may hold values from 2 to 256, as said below
Outputs:
- row_result: bfloat16 [2, 512, 8192], P('role', 'dp', 'tp')
The draws below stay inside these ranges and needn't reach their ends.
Inputs may be any that keep to these rules, and one draw needn't show every extreme that they name: `cache_len`: some row holds exactly 256 cached positions.
All inputs are finite; a program needn't handle non-finite values.
Results may differ from the reference program's by a relative error of at most 0.008.
Values may be sent and summed in bfloat16 or wider, within the bound.
A program may use at most 64 MiB of HBM per device.

```python
import math
import jax
import jax.numpy as jnp
from jax import lax

D = 8192
KVH = 8
QH = 64
HD = 128
STEPS = 8
ROWS_DEV = 16
CACHE = 256
TOKENS = 512
ROWS = 64
KVW = 1024
N_DP = 4
N_TP = 4


def shared_draw(key):
    base = jax.random.fold_in(key, 7)
    cache_keys = jnp.clip(jax.random.normal(jax.random.fold_in(base, 1), (ROWS, CACHE, KVH * HD), jnp.float32), -5.0, 5.0)
    query_vals = jnp.clip(2.0 * jax.random.normal(jax.random.fold_in(base, 2), (STEPS, ROWS, QH * HD), jnp.float32), -10.0, 10.0)
    return (query_vals, cache_keys)


def draw_queries(key, part):
    return shared_draw(key)[0].astype(jnp.bfloat16)


def draw_k_cache(key, part):
    return shared_draw(key)[1].astype(jnp.bfloat16)


def draw_cache_len(key, part):
    base = jax.random.fold_in(key, 31)
    wide_lengths = jax.random.randint(base, (ROWS,), 2, CACHE + 1, dtype=jnp.int32)
    short_top = max(CACHE // 8, 4)
    short_lengths = jax.random.randint(jax.random.fold_in(base, 2), (ROWS,), 2, short_top + 1, dtype=jnp.int32)
    picker = jax.random.randint(jax.random.fold_in(base, 3), (ROWS,), 0, 4, dtype=jnp.int32)
    lengths = jnp.where(picker == 0, wide_lengths, short_lengths)
    target = jax.random.randint(jax.random.fold_in(base, 1), (), 0, ROWS, dtype=jnp.int32)
    return lengths.at[target].set(CACHE)


def raised(values, rng, source, target, blocks, factor):
    def block_of(axis_at):
        return (jnp.arange(values.shape[axis_at]) // (values.shape[axis_at] // blocks)).reshape((-1,) + (1,) * (values.ndim - 1 - axis_at))

    near = jax.random.permutation(rng, blocks)[block_of(target)]
    other_side = (block_of(target) + blocks // 2) % blocks
    return jnp.where((block_of(source) == near) | (block_of(source) == other_side), factor * values, values)


def block_scale(rng, dims, pieces, low, largest):
    factor_of = 1.0
    for axis_at, blocks in pieces:
        steps = jax.random.uniform(jax.random.fold_in(jax.random.fold_in(rng, 6), axis_at), (blocks,), jnp.float32, low / len(pieces), largest / len(pieces))
        factor_of = factor_of * jnp.repeat(jnp.exp(steps), dims[axis_at] // blocks).reshape((-1,) + (1,) * (len(dims) - 1 - axis_at))
    return factor_of


def scatter_about(rng, extent, scale, most, shards=(), held_as=jnp.bfloat16):
    array = scale * jax.random.normal(rng, extent, jnp.float32)
    if shards:
        array = array * block_scale(rng, extent, shards, -0.22, 0.18)
    return jnp.clip(array, -most, most).astype(held_as)


def heavy_noise(stream_key, dims, scale, most, shards, heavy, kind=jnp.bfloat16):
    array = scale * jax.random.normal(stream_key, dims, jnp.float32)
    if shards:
        array = array * block_scale(stream_key, dims, shards, -0.22, 0.18)
    return jnp.clip(raised(array, jax.random.fold_in(stream_key, 3), *heavy), -most, most).astype(kind)


def setup_inputs(seed: int = 0) -> dict:
    seeds = jax.random.split(jax.random.key(seed), 11)
    hidden = heavy_noise(seeds[0], (2, TOKENS, D), 1.0, 6.0, ((0, 2), (1, 4)), (1, 2, 4, 2.0))
    out_grad = scatter_about(seeds[1], (TOKENS, KVW), 1.0, 6.0, ((0, 4), (1, 4)))
    master = scatter_about(seeds[2], (D, KVW), D ** -0.5, 0.0625, ((0, 4), (1, 4)), jnp.float32)
    moment1 = scatter_about(seeds[3], (D, KVW), 3.0, 18.0, ((0, 4), (1, 4)), jnp.float32)
    moment2 = jnp.clip(jnp.exp(math.log(500.0) - 2.3025851 * jax.random.uniform(seeds[4], (D, KVW), jnp.float32) ** block_scale(seeds[4], (D, KVW), ((0, 4), (1, 4)), -0.2, 0.2)), 50.0, 500.0)
    queries = draw_queries(jax.random.fold_in(seeds[10], 71), 0)
    new_keys = scatter_about(seeds[6], (STEPS, ROWS, KVW), 1.0, 6.0, ((1, 4), (2, 4)))
    k_cache = draw_k_cache(jax.random.fold_in(seeds[10], 71), 0)
    v_cache = scatter_about(seeds[8], (ROWS, CACHE, KVW), 1.0, 6.0, ((0, 4), (2, 4)))
    cache_len = draw_cache_len(jax.random.fold_in(seeds[10], 71), 0)
    return dict(hidden=hidden, out_grad=out_grad, master=master, moment1=moment1, moment2=moment2, queries=queries, new_keys=new_keys, k_cache=k_cache, v_cache=v_cache, cache_len=cache_len)


beta_one = 0.9
beta_two = 0.95
adam_eps = 1e-08
bias_one = 1.0 - 0.9 ** 10
bias_two = 1.0 - 0.95 ** 10
neg_fill = -1e+30

def adam_fresh(master, moment1, moment2, gradient):
    step_size = 2.0 * D ** (-0.5)
    first = beta_one * moment1 + (1.0 - beta_one) * gradient
    second = beta_two * moment2 + (1.0 - beta_two) * gradient * gradient
    change = first / bias_one / (jnp.sqrt(second / bias_two) + adam_eps)
    return (master - step_size * change).astype(jnp.bfloat16)

def attend_row(query_row, newkey_row, value_row, cache_keys, cache_vals, length):
    scale = HD ** (-0.5)
    cache_score = jnp.einsum('skgd,pkd->skgp', query_row.astype(jnp.float32), cache_keys.astype(jnp.float32)) * scale
    valid = jnp.arange(CACHE) < length
    cache_score = jnp.where(valid[None, None, None, :], cache_score, neg_fill)
    fresh_score = jnp.einsum('skgd,tkd->skgt', query_row.astype(jnp.float32), newkey_row.astype(jnp.float32)) * scale
    causal = jnp.arange(STEPS)[:, None] >= jnp.arange(STEPS)[None, :]
    fresh_score = jnp.where(causal[:, None, None, :], fresh_score, neg_fill)
    top = jnp.maximum(lax.optimization_barrier(jnp.max(cache_score, axis=-1)), lax.optimization_barrier(jnp.max(fresh_score, axis=-1)))
    cache_exp = jnp.exp(cache_score - top[..., None])
    fresh_exp = jnp.exp(fresh_score - top[..., None])
    total = lax.optimization_barrier(jnp.sum(cache_exp, axis=-1)) + lax.optimization_barrier(jnp.sum(fresh_exp, axis=-1))
    cache_wts = (cache_exp / total[..., None]).astype(jnp.bfloat16)
    fresh_wts = (fresh_exp / total[..., None]).astype(jnp.bfloat16)
    output = jnp.einsum('skgp,pkd->skgd', cache_wts.astype(jnp.float32), cache_vals.astype(jnp.float32))
    output = output + jnp.einsum('skgt,tkd->skgd', fresh_wts.astype(jnp.float32), value_row.astype(jnp.float32))
    return output.astype(jnp.bfloat16)

def reference(hidden, out_grad, master, moment1, moment2, queries, new_keys, k_cache, v_cache, cache_len):
    learn_in = hidden[0]
    roll_in = hidden[1]
    old_weight = master.astype(jnp.bfloat16)
    gradient = lax.dot_general(learn_in, out_grad, (((0,), (0,)), ((), ())), preferred_element_type=jnp.float32)
    span = KVH * HD // N_TP
    back_sum = jnp.zeros((TOKENS, D), jnp.float32)
    for group in range(N_TP):
        partial_value = jnp.dot(out_grad[:, group * span:(group + 1) * span], old_weight[:, group * span:(group + 1) * span].T, preferred_element_type=jnp.float32).astype(jnp.bfloat16)
        partial_value = lax.optimization_barrier(partial_value)
        back_sum = back_sum + partial_value.astype(jnp.float32)
    back_rows = back_sum.astype(jnp.bfloat16)
    fresh = adam_fresh(master, moment1, moment2, gradient)
    values = jnp.dot(roll_in, fresh, preferred_element_type=jnp.float32).astype(jnp.bfloat16)
    values = values.reshape(N_DP, STEPS, ROWS_DEV, KVH, HD).transpose(0, 2, 1, 3, 4).reshape(ROWS, STEPS, KVH, HD)
    query_all = queries.reshape(STEPS, ROWS, KVH, QH // KVH, HD).transpose(1, 0, 2, 3, 4)
    newkey_all = new_keys.reshape(STEPS, ROWS, KVH, HD).transpose(1, 0, 2, 3)
    cache_keys = k_cache.reshape(ROWS, CACHE, KVH, HD)
    cache_vals = v_cache.reshape(ROWS, CACHE, KVH, HD)

    def one_row(packed):
        return attend_row(packed[0], packed[1], packed[2], packed[3], packed[4], packed[5])
    attended = lax.map(one_row, (query_all, newkey_all, values, cache_keys, cache_vals, cache_len))
    attended = attended.reshape(N_DP, ROWS_DEV, STEPS, D).transpose(0, 2, 1, 3).reshape(TOKENS, D)
    return jnp.stack([back_rows, attended])
```

```python
import functools

import jax
import jax.numpy as jnp
from jax import lax
from jax.experimental import pallas as pl
from jax.experimental.pallas import tpu as pltpu
from jax.sharding import PartitionSpec as P

D = 8192
KVH = 8
QH = 64
HD = 128
STEPS = 8


beta_one = 0.9
beta_two = 0.95
adam_eps = 1e-08
bias_one = 1.0 - 0.9**10
bias_two = 1.0 - 0.95**10
neg_fill = -1e30


def adam_fresh(master, moment1, moment2, gradient):
    step_size = 2.0 * D ** (-0.5)
    first = beta_one * moment1 + (1.0 - beta_one) * gradient
    second = beta_two * moment2 + (1.0 - beta_two) * gradient * gradient
    change = first / bias_one / (jnp.sqrt(second / bias_two) + adam_eps)
    return (master - step_size * change).astype(jnp.bfloat16)


MESH = pl.DeviceIdType.MESH


def position():
    return lax.axis_index("role"), lax.axis_index("dp"), lax.axis_index("tp")


def signal(semaphore, role, row, col):
    pl.semaphore_signal(semaphore, inc=1, device_id=(role, row, col), device_id_type=MESH)


def remote(src, dst, send, recv, role, row, col):
    return pltpu.make_async_remote_copy(
        src_ref=src,
        dst_ref=dst,
        send_sem=send,
        recv_sem=recv,
        device_id=(role, row, col),
        device_id_type=MESH,
    )


def drain(ref, semaphore):
    pltpu.make_async_copy(ref, ref, semaphore).wait()


def each(count, body):
    def step(k, carry):
        body(k)
        return carry

    lax.fori_loop(0, count, step, 0)


def spread_kernel(
    n, m, hid, og, slabs, ogs,
    og_send, og_recv, hid_send, hid_recv, loc, x_send, x_recv, c_send, c_recv,
):
    r, i, t = position()
    rows, width = slabs.shape[3], slabs.shape[4]
    pairs = m // 2
    px, core = t // 2, t % 2

    barrier = pltpu.get_barrier_semaphore()

    def greet(k):
        @pl.when(k != r * n + i)
        def _():
            signal(barrier, k // n, k % n, t)

    def greet_tp(k):
        @pl.when(k != t)
        def _():
            signal(barrier, r, i, k)

    each(2 * n, greet)
    each(m, greet_tp)
    pl.semaphore_wait(barrier, 2 * n - 1 + m - 1)

    def piece(j):
        return hid.at[pl.ds(pl.multiple_of(t * rows, rows), rows), pl.ds(pl.multiple_of(j * width, width), width)]

    def send_og(k):
        j = (i + k) % n
        remote(og, ogs.at[i], og_send, og_recv, r, j, t).start()

    def send_hid(k):
        j = (i + k) % n
        remote(piece(j), slabs.at[r, t, i], hid_send, hid_recv.at[r], 1, j, t).start()

    each(n - 1, lambda k: send_og(k + 1))
    each(n - 1, lambda k: send_hid(k + 1))
    og_local = pltpu.make_async_copy(og, ogs.at[i], loc.at[0])
    og_local.start()

    @pl.when(r == 0)
    def _():
        send_hid(0)

    @pl.when(r == 1)
    def _():
        own = pltpu.make_async_copy(piece(i), slabs.at[1, t, i], loc.at[1])
        own.start()

        def to_pair(which, src):
            return remote(
                slabs.at[which, src * 2 + core],
                slabs.at[which, src * 2 + core],
                c_send.at[which, src],
                c_recv.at[which, src],
                1, i, t + 1 - 2 * core,
            )

        def from_pair(which, src):
            drain(slabs.at[which, src * 2 + 1 - core], c_recv.at[which, src])

        def over(which, step):
            dst = (px + step) % pairs
            return remote(
                slabs.at[which, t],
                slabs.at[which, t],
                x_send.at[which, step],
                x_recv.at[which, px],
                1, i, dst * 2 + core,
            )

        for which in range(2):
            if which == 0:
                drain(slabs.at[0, t], hid_recv.at[0])
            else:
                drain(slabs.at[1, t, pl.ds(0, n - 1)], hid_recv.at[1])
                own.wait()
            for step in range(1, pairs):
                over(which, step).start()
            to_pair(which, px).start()
        for which in range(2):
            for step in range(1, pairs):
                src = (px + step) % pairs
                drain(slabs.at[which, src * 2 + core], x_recv.at[which, src])
                to_pair(which, src).start()
        for which in range(2):
            for src in range(pairs):
                from_pair(which, src)
        for which in range(2):
            for step in range(1, pairs):
                over(which, step).wait_send()
            for src in range(pairs):
                to_pair(which, src).wait_send()
        drain(slabs.at[1, t, pl.ds(0, n - 1)], hid_send)

    @pl.when(r == 0)
    def _():
        drain(slabs.at[1, t], hid_send)

    drain(ogs.at[pl.ds(0, n - 1)], og_send)
    drain(ogs.at[pl.ds(0, n - 1)], og_recv)
    og_local.wait()


def spread(hid, og, n, m):
    rows, width = hid.shape[0] // m, hid.shape[1] // n
    dma = pltpu.SemaphoreType.DMA
    anywhere = pl.BlockSpec(memory_space=pl.ANY)
    return pl.pallas_call(
        functools.partial(spread_kernel, n, m),
        out_shape=(
            jax.ShapeDtypeStruct((2, m, n, rows, width), hid.dtype),
            jax.ShapeDtypeStruct((n,) + og.shape, og.dtype),
        ),
        in_specs=[anywhere] * 2,
        out_specs=(anywhere, anywhere),
        scratch_shapes=[
            dma, dma, dma, dma((2,)), dma((2,)),
            dma((2, m // 2)), dma((2, m // 2)), dma((2, m // 2)), dma((2, m // 2)),
        ],
        compiler_params=pltpu.CompilerParams(collective_id=0, has_side_effects=True),
    )(hid, og)


def total_of(slots, count, out, tile):
    def chunk(k):
        at = pl.ds(pl.multiple_of(k * tile, tile), tile)
        total = slots[0, at, :].astype(jnp.float32)
        for s in range(1, count):
            total = total + slots[s, at, :].astype(jnp.float32)
        out[at, :] = total.astype(out.dtype)

    each(out.shape[0] // tile, chunk)


def collect_kernel(
    n, m, parts, sums, back, vals,
    slots, reduced, val_slots, own_sem, p_send, p_recv, b_send, b_recv, v_send, v_recv,
):
    r, i, t = position()
    q = n // m
    width = parts.shape[2]
    rows = back.shape[0]
    home = i // q

    barrier = pltpu.get_barrier_semaphore()

    @pl.when(r == 0)
    def _():
        def greet_tp(k):
            signal(barrier, 0, i, (t + 1 + k) % m)

        def greet_far(k):
            @pl.when(t * q + k != i)
            def _():
                signal(barrier, 0, t * q + k, home)

        each(m - 1, greet_tp)
        each(q, greet_far)
        at_home = jnp.where(home == t, 1, 0)
        pl.semaphore_wait(barrier, m - 1 + q - at_home)

        def send_part(k):
            g = (t + 1 + k) % m
            remote(parts.at[g], slots.at[t], p_send, p_recv, 0, i, g).start()

        each(m - 1, send_part)
        mine = pltpu.make_async_copy(parts.at[t], slots.at[t], own_sem)
        mine.start()
        drain(slots.at[pl.ds(0, m - 1)], p_recv)
        mine.wait()
        total_of(slots, m, reduced, 16)

        def place(j):
            return back.at[:, pl.ds(pl.multiple_of((j % q) * width, width), width)]

        def block(k):
            return reduced.at[pl.ds(pl.multiple_of(k * rows, rows), rows)]

        def send_block(k):
            @pl.when(t * q + k != i)
            def _():
                remote(block(k), place(i), b_send, b_recv, 0, t * q + k, home).start()

        each(q, send_block)

        @pl.when(home == t)
        def _():
            keep = pltpu.make_async_copy(block(i % q), place(i), own_sem)
            keep.start()
            keep.wait()
            if q > 1:
                drain(reduced.at[pl.ds(0, (q - 1) * rows)], b_recv)
                drain(reduced.at[pl.ds(0, (q - 1) * rows)], b_send)

        @pl.when(home != t)
        def _():
            drain(reduced, b_recv)
            drain(reduced, b_send)

        drain(slots.at[pl.ds(0, m - 1)], p_send)

    @pl.when(r == 1)
    def _():
        def greet_dp(k):
            signal(barrier, 1, (i + 1 + k) % n, t)

        each(n - 1, greet_dp)
        pl.semaphore_wait(barrier, n - 1)

        def send_sum(k):
            j = (i + 1 + k) % n
            remote(sums.at[j], val_slots.at[i], v_send, v_recv, 1, j, t).start()

        each(n - 1, send_sum)
        mine = pltpu.make_async_copy(sums.at[i], val_slots.at[i], own_sem)
        mine.start()
        drain(val_slots.at[pl.ds(0, n - 1)], v_recv)
        mine.wait()
        total_of(val_slots, n, vals, 16)
        drain(val_slots.at[pl.ds(0, n - 1)], v_send)


def collect(parts, sums, n, m):
    q = n // m
    rows, width = parts.shape[1] // q, parts.shape[2]
    dma = pltpu.SemaphoreType.DMA
    anywhere = pl.BlockSpec(memory_space=pl.ANY)
    return pl.pallas_call(
        functools.partial(collect_kernel, n, m),
        out_shape=(
            jax.ShapeDtypeStruct((rows, q * width), jnp.bfloat16),
            jax.ShapeDtypeStruct(sums.shape[1:], jnp.bfloat16),
        ),
        in_specs=[anywhere] * 2,
        out_specs=(anywhere, pl.BlockSpec(memory_space=pltpu.VMEM)),
        scratch_shapes=[
            pltpu.VMEM(parts.shape, jnp.bfloat16),
            pltpu.VMEM(parts.shape[1:], jnp.bfloat16),
            pltpu.VMEM(sums.shape, jnp.bfloat16),
            dma, dma, dma, dma, dma, dma, dma,
        ],
        compiler_params=pltpu.CompilerParams(
            collective_id=1, has_side_effects=True, vmem_limit_bytes=16 * 2**20
        ),
    )(parts, sums)


def local(
    hidden, out_grad, master, moment1, moment2, queries, new_keys, k_cache, v_cache, cache_len
):
    group_index = lax.axis_index("role")
    is_learner = group_index == 0
    own_rows = hidden[0]
    width_here = out_grad.shape[1]
    heads_here = width_here // HD
    share = QH // KVH
    replica_rows = cache_len.shape[0]
    cache_size = k_cache.shape[1]
    n, m = lax.axis_size("dp"), lax.axis_size("tp")
    slabs, ogs = spread(own_rows, out_grad, n, m)
    rows, width = slabs.shape[3], slabs.shape[4]
    grads = ogs.reshape(n, m, rows, width_here).transpose(1, 0, 2, 3)
    gradient = lax.dot_general(
        slabs[0].reshape(n * m * rows, width),
        grads.reshape(n * m * rows, width_here),
        (((0,), (0,)), ((), ())),
        preferred_element_type=jnp.float32,
    )
    fresh = adam_fresh(master, moment1, moment2, gradient)
    old_weight = master.astype(jnp.bfloat16)
    parts = lax.dot_general(
        ogs.reshape(n * m * rows, width_here),
        old_weight,
        (((1,), (1,)), ((), ())),
        preferred_element_type=jnp.float32,
    ).astype(jnp.bfloat16)
    sums = jnp.dot(
        slabs[1].reshape(n * m * rows, width), fresh, preferred_element_type=jnp.float32
    ).astype(jnp.bfloat16)
    sums = sums.reshape(m, n, rows, width_here).transpose(1, 0, 2, 3).reshape(n, m * rows, width_here)
    learner_rows, values = collect(parts.reshape(m, n * rows, width), sums, n, m)
    values = values.reshape(STEPS, replica_rows, heads_here, HD)
    query_all = queries.reshape(STEPS, replica_rows, heads_here, share, HD)
    newkey_all = new_keys.reshape(STEPS, replica_rows, heads_here, HD)
    cache_keys = k_cache.reshape(replica_rows, cache_size, heads_here, HD)
    cache_vals = v_cache.reshape(replica_rows, cache_size, heads_here, HD)
    scale = HD ** (-0.5)
    cache_score = (
        jnp.einsum("srkgd,rpkd->srkgp", query_all, cache_keys, preferred_element_type=jnp.float32)
        * scale
    )
    valid = jnp.arange(cache_size)[None, :] < cache_len[:, None]
    cache_score = jnp.where(valid[None, :, None, None, :], cache_score, neg_fill)
    fresh_score = (
        jnp.einsum("srkgd,trkd->srkgt", query_all, newkey_all, preferred_element_type=jnp.float32)
        * scale
    )
    causal = jnp.arange(STEPS)[:, None] >= jnp.arange(STEPS)[None, :]
    fresh_score = jnp.where(causal[:, None, None, None, :], fresh_score, neg_fill)
    top = jnp.maximum(jnp.max(cache_score, axis=-1), jnp.max(fresh_score, axis=-1))
    cache_exp = jnp.exp(cache_score - top[..., None])
    fresh_exp = jnp.exp(fresh_score - top[..., None])
    total = jnp.sum(cache_exp, axis=-1) + jnp.sum(fresh_exp, axis=-1)
    cache_wts = (cache_exp / total[..., None]).astype(jnp.bfloat16)
    fresh_wts = (fresh_exp / total[..., None]).astype(jnp.bfloat16)
    output = jnp.einsum(
        "srkgp,rpkd->srkgd", cache_wts, cache_vals, preferred_element_type=jnp.float32
    )
    output = output + jnp.einsum(
        "srkgt,trkd->srkgd", fresh_wts, values, preferred_element_type=jnp.float32
    )
    decoded = output.astype(jnp.bfloat16).reshape(STEPS * replica_rows, heads_here * share * HD)
    result = jnp.where(is_learner, learner_rows, decoded)
    return result[None]


def solution(mesh):
    return jax.shard_map(
        local,
        mesh=mesh,
        in_specs=(
            P("role", "dp", None),
            P("dp", "tp"),
            P("dp", "tp"),
            P("dp", "tp"),
            P("dp", "tp"),
            P(None, "dp", "tp"),
            P(None, "dp", "tp"),
            P("dp", None, "tp"),
            P("dp", None, "tp"),
            P("dp"),
        ),
        out_specs=P("role", "dp", "tp"),
        check_vma=False,
    )
```

```python
import functools

import jax
import jax.numpy as jnp
from jax import lax
from jax.experimental import pallas as pl
from jax.experimental.pallas import tpu as pltpu
from jax.sharding import PartitionSpec as P

D = 8192
KVH = 8
QH = 64
HD = 128
STEPS = 8


beta_one = 0.9
beta_two = 0.95
adam_eps = 1e-08
bias_one = 1.0 - 0.9**10
bias_two = 1.0 - 0.95**10
neg_fill = -1e30


def adam_fresh(master, moment1, moment2, gradient):
    step_size = 2.0 * D ** (-0.5)
    first = beta_one * moment1 + (1.0 - beta_one) * gradient
    second = beta_two * moment2 + (1.0 - beta_two) * gradient * gradient
    change = first / bias_one / (jnp.sqrt(second / bias_two) + adam_eps)
    return (master - step_size * change).astype(jnp.bfloat16)


MESH = pl.DeviceIdType.MESH


def position():
    return lax.axis_index("role"), lax.axis_index("dp"), lax.axis_index("tp")


def signal(semaphore, role, row, col):
    pl.semaphore_signal(semaphore, inc=1, device_id=(role, row, col), device_id_type=MESH)


def remote(src, dst, send, recv, role, row, col):
    return pltpu.make_async_remote_copy(
        src_ref=src,
        dst_ref=dst,
        send_sem=send,
        recv_sem=recv,
        device_id=(role, row, col),
        device_id_type=MESH,
    )


def drain(ref, semaphore):
    pltpu.make_async_copy(ref, ref, semaphore).wait()


def each(count, body):
    def step(k, carry):
        body(k)
        return carry

    lax.fori_loop(0, count, step, 0)


def spread_kernel(
    n, m, split, hid, og, slabs, ogs,
    og_send, og_recv, hid_send, hid_recv, loc, x_send, x_recv, c_send, c_recv,
):
    r, i, t = position()
    rows, width = slabs.shape[3], slabs.shape[4]
    pairs = m // 2
    px, core = t // 2, t % 2

    barrier = pltpu.get_barrier_semaphore()

    def greet(k):
        @pl.when(k != r * n + i)
        def _():
            signal(barrier, k // n, k % n, t)

    def greet_tp(k):
        @pl.when(k != t)
        def _():
            signal(barrier, r, i, k)

    each(2 * n, greet)
    each(m, greet_tp)
    pl.semaphore_wait(barrier, 2 * n - 1 + m - 1)

    full = hid.shape[1] // n

    def piece(role, j):
        start = j * full + (role * width if split else 0)
        return hid.at[pl.ds(pl.multiple_of(t * rows, rows), rows), pl.ds(pl.multiple_of(start, width), width)]

    def send_og(k):
        j = (i + k) % n
        remote(og, ogs.at[i], og_send, og_recv, r, j, t).start()

    def send_hid(role, j):
        remote(piece(role, j), slabs.at[r, t, i], hid_send.at[role], hid_recv.at[r], role, j, t).start()

    each(n - 1, lambda k: send_og(k + 1))
    targets = (0, 1) if split else (1,)
    for role in targets:
        each(n - 1, lambda k, role=role: send_hid(role, (i + k + 1) % n))

        @pl.when(r != role)
        def _(role=role):
            send_hid(role, i)

    og_local = pltpu.make_async_copy(og, ogs.at[i], loc.at[0])
    og_local.start()

    @pl.when((r == 1) | split)
    def _():
        own = pltpu.make_async_copy(piece(r, i), slabs.at[r, t, i], loc.at[1])
        own.start()

        def to_pair(which, src):
            return remote(
                slabs.at[which, src * 2 + core],
                slabs.at[which, src * 2 + core],
                c_send.at[which, src],
                c_recv.at[which, src],
                r, i, t + 1 - 2 * core,
            )

        def from_pair(which, src):
            drain(slabs.at[which, src * 2 + 1 - core], c_recv.at[which, src])

        def over(which, step):
            dst = (px + step) % pairs
            return remote(
                slabs.at[which, t],
                slabs.at[which, t],
                x_send.at[which, step],
                x_recv.at[which, px],
                r, i, dst * 2 + core,
            )

        for which in range(2):
            @pl.when(r != which)
            def _(which=which):
                drain(slabs.at[which, t], hid_recv.at[which])

            @pl.when(r == which)
            def _(which=which):
                drain(slabs.at[which, t, pl.ds(0, n - 1)], hid_recv.at[which])
                own.wait()

            for step in range(1, pairs):
                over(which, step).start()
            to_pair(which, px).start()
        for which in range(2):
            for step in range(1, pairs):
                src = (px + step) % pairs
                drain(slabs.at[which, src * 2 + core], x_recv.at[which, src])
                to_pair(which, src).start()
        for which in range(2):
            for src in range(pairs):
                from_pair(which, src)
        for which in range(2):
            for step in range(1, pairs):
                over(which, step).wait_send()
            for src in range(pairs):
                to_pair(which, src).wait_send()

    for role in targets:
        @pl.when(r != role)
        def _(role=role):
            drain(slabs.at[role, t], hid_send.at[role])

        @pl.when(r == role)
        def _(role=role):
            drain(slabs.at[role, t, pl.ds(0, n - 1)], hid_send.at[role])

    drain(ogs.at[pl.ds(0, n - 1)], og_send)
    drain(ogs.at[pl.ds(0, n - 1)], og_recv)
    og_local.wait()


def spread(hid, og, n, m, split):
    rows, width = hid.shape[0] // m, hid.shape[1] // n // (2 if split else 1)
    dma = pltpu.SemaphoreType.DMA
    anywhere = pl.BlockSpec(memory_space=pl.ANY)
    return pl.pallas_call(
        functools.partial(spread_kernel, n, m, split),
        out_shape=(
            jax.ShapeDtypeStruct((2, m, n, rows, width), hid.dtype),
            jax.ShapeDtypeStruct((n,) + og.shape, og.dtype),
        ),
        in_specs=[anywhere] * 2,
        out_specs=(anywhere, anywhere),
        scratch_shapes=[
            dma, dma, dma((2,)), dma((2,)), dma((2,)),
            dma((2, m // 2)), dma((2, m // 2)), dma((2, m // 2)), dma((2, m // 2)),
        ],
        compiler_params=pltpu.CompilerParams(collective_id=0, has_side_effects=True),
    )(hid, og)


def total_of(slots, count, out, tile):
    def chunk(k):
        at = pl.ds(pl.multiple_of(k * tile, tile), tile)
        total = slots[0, at, :].astype(jnp.float32)
        for s in range(1, count):
            total = total + slots[s, at, :].astype(jnp.float32)
        out[at, :] = total.astype(out.dtype)

    each(out.shape[0] // tile, chunk)


def collect_kernel(
    n, m, split, ogs, master, sums, back, vals,
    parts, slots, reduced, val_slots, own_sem, p_send, p_recv, b_send, b_recv, v_send, v_recv,
):
    r, i, t = position()
    q = n // m
    width = parts.shape[2]
    rows = back.shape[0]
    home = i // q
    chunk = min(512, width)
    sources = val_slots.shape[0]

    def send_sum(j):
        slot = r * n + i if split else i
        remote(sums.at[j], val_slots.at[slot], v_send, v_recv, 1, j, t).start()

    def fill_part(g):
        def columns(k):
            at = pl.ds(pl.multiple_of(k * chunk, chunk), chunk)
            parts[g, :, at] = lax.dot_general(
                ogs[g],
                master[at, :].astype(jnp.bfloat16),
                (((1,), (1,)), ((), ())),
                preferred_element_type=jnp.float32,
            ).astype(jnp.bfloat16)

        each(width // chunk, columns)

    barrier = pltpu.get_barrier_semaphore()

    @pl.when(r == 0)
    def _():
        def greet_tp(k):
            signal(barrier, 0, i, (t + 1 + k) % m)

        def greet_far(k):
            @pl.when(t * q + k != i)
            def _():
                signal(barrier, 0, t * q + k, home)

        each(m - 1, greet_tp)
        each(q, greet_far)
        at_home = jnp.where(home == t, 1, 0)
        pl.semaphore_wait(barrier, m - 1 + q - at_home + (n if split else 0))
        if split:
            each(n, lambda k: send_sum((i + k) % n))

        def send_part(k):
            g = (t + 1 + k) % m
            fill_part(g)
            remote(parts.at[g], slots.at[t], p_send, p_recv, 0, i, g).start()

        each(m - 1, send_part)
        fill_part(t)
        mine = pltpu.make_async_copy(parts.at[t], slots.at[t], own_sem)
        mine.start()
        drain(slots.at[pl.ds(0, m - 1)], p_recv)
        mine.wait()
        total_of(slots, m, reduced, 16)

        def place(j):
            return back.at[:, pl.ds(pl.multiple_of((j % q) * width, width), width)]

        def block(k):
            return reduced.at[pl.ds(pl.multiple_of(k * rows, rows), rows)]

        def send_block(k):
            @pl.when(t * q + k != i)
            def _():
                remote(block(k), place(i), b_send, b_recv, 0, t * q + k, home).start()

        each(q, send_block)

        @pl.when(home == t)
        def _():
            keep = pltpu.make_async_copy(block(i % q), place(i), own_sem)
            keep.start()
            keep.wait()
            if q > 1:
                drain(reduced.at[pl.ds(0, (q - 1) * rows)], b_recv)
                drain(reduced.at[pl.ds(0, (q - 1) * rows)], b_send)

        @pl.when(home != t)
        def _():
            drain(reduced, b_recv)
            drain(reduced, b_send)

        drain(slots.at[pl.ds(0, m - 1)], p_send)
        if split:
            drain(val_slots.at[pl.ds(0, n)], v_send)

    @pl.when(r == 1)
    def _():
        def greet_dp(k):
            signal(barrier, 1, (i + 1 + k) % n, t)

        each(n - 1, greet_dp)
        if split:
            each(n, lambda k: signal(barrier, 0, k, t))
        pl.semaphore_wait(barrier, n - 1)
        each(n - 1, lambda k: send_sum((i + 1 + k) % n))
        mine = pltpu.make_async_copy(sums.at[i], val_slots.at[n + i if split else i], own_sem)
        mine.start()
        drain(val_slots.at[pl.ds(0, sources - 1)], v_recv)
        mine.wait()
        total_of(val_slots, sources, vals, 16)
        drain(val_slots.at[pl.ds(0, n - 1)], v_send)


def collect(ogs, master, sums, n, m, split):
    q = n // m
    rows, width = ogs.shape[1] // q, master.shape[0]
    parts = pltpu.VMEM((m, q * rows, width), jnp.bfloat16)
    dma = pltpu.SemaphoreType.DMA
    anywhere = pl.BlockSpec(memory_space=pl.ANY)
    inside = pl.BlockSpec(memory_space=pltpu.VMEM)
    return pl.pallas_call(
        functools.partial(collect_kernel, n, m, split),
        out_shape=(
            jax.ShapeDtypeStruct((rows, q * width), jnp.bfloat16),
            jax.ShapeDtypeStruct(sums.shape[1:], jnp.bfloat16),
        ),
        in_specs=[inside, inside, anywhere],
        out_specs=(anywhere, inside),
        scratch_shapes=[
            parts,
            parts,
            pltpu.VMEM((q * rows, width), jnp.bfloat16),
            pltpu.VMEM((n * (2 if split else 1),) + sums.shape[1:], jnp.bfloat16),
            dma, dma, dma, dma, dma, dma, dma,
        ],
        compiler_params=pltpu.CompilerParams(
            collective_id=1, has_side_effects=True, vmem_limit_bytes=32 * 2**20
        ),
    )(ogs, master, sums)


def local(
    hidden, out_grad, master, moment1, moment2, queries, new_keys, k_cache, v_cache, cache_len
):
    group_index = lax.axis_index("role")
    is_learner = group_index == 0
    own_rows = hidden[0]
    width_here = out_grad.shape[1]
    n, m = lax.axis_size("dp"), lax.axis_size("tp")
    split = (own_rows.shape[1] // n) % 256 == 0
    slabs, ogs = spread(own_rows, out_grad, n, m, split)
    rows, width = slabs.shape[3], slabs.shape[4]
    grads = ogs.reshape(n, m, rows, width_here).transpose(1, 0, 2, 3)
    gradient = lax.dot_general(
        slabs[0].reshape(n * m * rows, width),
        grads.reshape(n * m * rows, width_here),
        (((0,), (0,)), ((), ())),
        preferred_element_type=jnp.float32,
    )
    first_row = group_index * width if split else 0
    mine = [
        lax.dynamic_slice_in_dim(a, first_row, width, axis=0) for a in (master, moment1, moment2)
    ]
    fresh = adam_fresh(*mine, gradient)
    sums = jnp.dot(
        slabs[1].reshape(n * m * rows, width), fresh, preferred_element_type=jnp.float32
    ).astype(jnp.bfloat16)
    sums = sums.reshape(m, n, rows, width_here).transpose(1, 0, 2, 3).reshape(n, m * rows, width_here)
    learner_rows, values = collect(
        ogs.reshape(m, n * rows, width_here), master, sums, n, m, split
    )
    result = lax.cond(
        is_learner,
        lambda: learner_rows,
        lambda: attend(values, queries, new_keys, k_cache, v_cache, cache_len),
    )
    return result[None]


def attend(values, queries, new_keys, k_cache, v_cache, cache_len):
    heads_here = values.shape[1] // HD
    share = QH // KVH
    replica_rows = cache_len.shape[0]
    cache_size = k_cache.shape[1]
    values = values.reshape(STEPS, replica_rows, heads_here, HD)
    query_all = queries.reshape(STEPS, replica_rows, heads_here, share, HD)
    newkey_all = new_keys.reshape(STEPS, replica_rows, heads_here, HD)
    cache_keys = k_cache.reshape(replica_rows, cache_size, heads_here, HD)
    cache_vals = v_cache.reshape(replica_rows, cache_size, heads_here, HD)
    scale = HD ** (-0.5)
    cache_score = (
        jnp.einsum("srkgd,rpkd->srkgp", query_all, cache_keys, preferred_element_type=jnp.float32)
        * scale
    )
    valid = jnp.arange(cache_size)[None, :] < cache_len[:, None]
    cache_score = jnp.where(valid[None, :, None, None, :], cache_score, neg_fill)
    fresh_score = (
        jnp.einsum("srkgd,trkd->srkgt", query_all, newkey_all, preferred_element_type=jnp.float32)
        * scale
    )
    causal = jnp.arange(STEPS)[:, None] >= jnp.arange(STEPS)[None, :]
    fresh_score = jnp.where(causal[:, None, None, None, :], fresh_score, neg_fill)
    top = jnp.maximum(jnp.max(cache_score, axis=-1), jnp.max(fresh_score, axis=-1))
    cache_exp = jnp.exp(cache_score - top[..., None])
    fresh_exp = jnp.exp(fresh_score - top[..., None])
    total = jnp.sum(cache_exp, axis=-1) + jnp.sum(fresh_exp, axis=-1)
    cache_wts = (cache_exp / total[..., None]).astype(jnp.bfloat16)
    fresh_wts = (fresh_exp / total[..., None]).astype(jnp.bfloat16)
    output = jnp.einsum(
        "srkgp,rpkd->srkgd", cache_wts, cache_vals, preferred_element_type=jnp.float32
    )
    output = output + jnp.einsum(
        "srkgt,trkd->srkgd", fresh_wts, values, preferred_element_type=jnp.float32
    )
    return output.astype(jnp.bfloat16).reshape(STEPS * replica_rows, heads_here * share * HD)


def solution(mesh):
    return jax.shard_map(
        local,
        mesh=mesh,
        in_specs=(
            P("role", "dp", None),
            P("dp", "tp"),
            P("dp", "tp"),
            P("dp", "tp"),
            P("dp", "tp"),
            P(None, "dp", "tp"),
            P(None, "dp", "tp"),
            P("dp", None, "tp"),
            P("dp", None, "tp"),
            P("dp"),
        ),
        out_specs=P("role", "dp", "tp"),
        check_vma=False,
    )
```

```python
import functools

import jax
import jax.numpy as jnp
from jax import lax
from jax.experimental import pallas as pl
from jax.experimental.pallas import tpu as pltpu
from jax.sharding import PartitionSpec as P

D = 8192
KVH = 8
QH = 64
HD = 128
STEPS = 8


beta_one = 0.9
beta_two = 0.95
adam_eps = 1e-08
bias_one = 1.0 - 0.9**10
bias_two = 1.0 - 0.95**10
neg_fill = -1e30


def adam_fresh(master, moment1, moment2, gradient):
    step_size = 2.0 * D ** (-0.5)
    first = beta_one * moment1 + (1.0 - beta_one) * gradient
    second = beta_two * moment2 + (1.0 - beta_two) * gradient * gradient
    change = first / bias_one / (jnp.sqrt(second / bias_two) + adam_eps)
    return (master - step_size * change).astype(jnp.bfloat16)


MESH = pl.DeviceIdType.MESH


def position():
    return lax.axis_index("role"), lax.axis_index("dp"), lax.axis_index("tp")


def signal(semaphore, role, row, col):
    pl.semaphore_signal(semaphore, inc=1, device_id=(role, row, col), device_id_type=MESH)


def remote(src, dst, send, recv, role, row, col):
    return pltpu.make_async_remote_copy(
        src_ref=src,
        dst_ref=dst,
        send_sem=send,
        recv_sem=recv,
        device_id=(role, row, col),
        device_id_type=MESH,
    )


def drain(ref, semaphore):
    pltpu.make_async_copy(ref, ref, semaphore).wait()


def each(count, body):
    def step(k, carry):
        body(k)
        return carry

    lax.fori_loop(0, count, step, 0)


def total_of(slots, count, out, tile):
    def chunk(k):
        at = pl.ds(pl.multiple_of(k * tile, tile), tile)
        total = slots[0, at, :].astype(jnp.float32)
        for s in range(1, count):
            total = total + slots[s, at, :].astype(jnp.float32)
        out[at, :] = total.astype(out.dtype)

    each(out.shape[0] // tile, chunk)


def fused_kernel(
    n, m, split, hid, og, master, moment1, moment2, back, vals,
    slabs, ogs, master_v, moment1_v, moment2_v, fresh, sums, parts, slots, reduced, val_slots,
    og_send, og_recv, hid_send, hid_recv, loc, x_send, x_recv, c_send, c_recv,
    p_send, p_recv, b_send, b_recv, v_send, v_recv,
):
    r, i, t = position()
    q = n // m
    rows, width = slabs.shape[3], slabs.shape[4]
    full = master.shape[0]
    heads = og.shape[1]
    home = i // q
    pairs = m // 2
    px, core = t // 2, t % 2
    sources = val_slots.shape[0]
    active = (r == 1) | split

    loads = [pltpu.make_async_copy(master, master_v, loc.at[2])]
    first = pl.multiple_of((r * width) if split else 0, width)
    for k, (src, dst) in enumerate(((moment1, moment1_v), (moment2, moment2_v))):
        loads.append(pltpu.make_async_copy(src.at[pl.ds(first, width)], dst, loc.at[3 + k]))
    for load in loads:
        load.start()

    barrier = pltpu.get_barrier_semaphore()

    def greet(k):
        @pl.when(k != r * n + i)
        def _():
            signal(barrier, k // n, k % n, t)

    def greet_tp(k):
        signal(barrier, r, i, (t + 1 + k) % m)

    def greet_far(k):
        @pl.when(t * q + k != i)
        def _():
            signal(barrier, 0, t * q + k, home)

    each(2 * n, greet)
    each(m - 1, greet_tp)

    @pl.when(r == 0)
    def _():
        each(q, greet_far)
        pl.semaphore_wait(barrier, 2 * n - 1 + m - 1 + q - jnp.where(home == t, 1, 0))

    @pl.when(r == 1)
    def _():
        pl.semaphore_wait(barrier, 2 * n - 1 + m - 1)

    def piece(role, j):
        start = j * full + (role * width if split else 0)
        return hid.at[pl.ds(pl.multiple_of(t * rows, rows), rows), pl.ds(pl.multiple_of(start, width), width)]

    def send_og(k):
        j = (i + k) % n
        remote(og, ogs.at[i], og_send, og_recv, r, j, t).start()

    def send_hid(role, j):
        remote(piece(role, j), slabs.at[r, t, i], hid_send.at[role], hid_recv.at[r], role, j, t).start()

    each(n - 1, lambda k: send_og(k + 1))
    targets = (0, 1) if split else (1,)
    for role in targets:
        each(n - 1, lambda k, role=role: send_hid(role, (i + k + 1) % n))

        @pl.when(r != role)
        def _(role=role):
            send_hid(role, i)

    og_local = pltpu.make_async_copy(og, ogs.at[i], loc.at[0])
    og_local.start()

    def to_pair(which, src):
        return remote(
            slabs.at[which, src * 2 + core],
            slabs.at[which, src * 2 + core],
            c_send.at[which, src],
            c_recv.at[which, src],
            r, i, t + 1 - 2 * core,
        )

    def from_pair(which, src):
        drain(slabs.at[which, src * 2 + 1 - core], c_recv.at[which, src])

    def over(which, step):
        dst = (px + step) % pairs
        return remote(
            slabs.at[which, t],
            slabs.at[which, t],
            x_send.at[which, step],
            x_recv.at[which, px],
            r, i, dst * 2 + core,
        )

    @pl.when(active)
    def _():
        own = pltpu.make_async_copy(piece(r, i), slabs.at[r, t, i], loc.at[1])
        own.start()
        for which in range(2):
            @pl.when(r != which)
            def _(which=which):
                drain(slabs.at[which, t], hid_recv.at[which])

            @pl.when(r == which)
            def _(which=which):
                drain(slabs.at[which, t, pl.ds(0, n - 1)], hid_recv.at[which])
                own.wait()

            for step in range(1, pairs):
                over(which, step).start()
            to_pair(which, px).start()

    drain(ogs.at[pl.ds(0, n - 1)], og_recv)
    og_local.wait()
    for load in loads:
        load.wait()

    chunk = min(512, full)
    block_rows = q * og.shape[0]

    def fill_part(g):
        tokens = ogs[pl.ds(g * q, q)].reshape(block_rows, heads)

        def columns(k):
            at = pl.ds(pl.multiple_of(k * chunk, chunk), chunk)
            parts[g, :, at] = lax.dot_general(
                tokens,
                master_v[at, :].astype(jnp.bfloat16),
                (((1,), (1,)), ((), ())),
                preferred_element_type=jnp.float32,
            ).astype(jnp.bfloat16)

        each(full // chunk, columns)

    mine = pltpu.make_async_copy(parts.at[t], slots.at[t], loc.at[0])

    @pl.when(r == 0)
    def _():
        def send_part(k):
            g = (t + 1 + k) % m
            fill_part(g)
            remote(parts.at[g], slots.at[t], p_send, p_recv, 0, i, g).start()

        each(m - 1, send_part)
        fill_part(t)
        mine.start()

    def send_sum(j):
        slot = r * n + i if split else i
        remote(sums.at[j], val_slots.at[slot], v_send, v_recv, 1, j, t).start()

    @pl.when(active)
    def _():
        for which in range(2):
            for step in range(1, pairs):
                src = (px + step) % pairs
                drain(slabs.at[which, src * 2 + core], x_recv.at[which, src])
                to_pair(which, src).start()
        for src in range(pairs):
            from_pair(0, src)

        tile = min(256, width)

        def update(k):
            at = pl.ds(pl.multiple_of(k * tile, tile), tile)
            gradient = jnp.zeros((tile, heads), jnp.float32)
            for g in range(m):
                gradient = gradient + lax.dot_general(
                    slabs[0, g, :, :, at].reshape(n * rows, tile),
                    ogs[:, g * rows : (g + 1) * rows, :].reshape(n * rows, heads),
                    (((0,), (0,)), ((), ())),
                    preferred_element_type=jnp.float32,
                )
            held = pl.ds(pl.multiple_of(first + k * tile, tile), tile)
            fresh[at, :] = adam_fresh(master_v[held, :], moment1_v[at, :], moment2_v[at, :], gradient)

        each(width // tile, update)
        for src in range(pairs):
            from_pair(1, src)
        for g in range(m):
            sums[:, g * rows : (g + 1) * rows, :] = (
                jnp.dot(
                    slabs[1, g].reshape(n * rows, width), fresh[...], preferred_element_type=jnp.float32
                )
                .astype(jnp.bfloat16)
                .reshape(n, rows, heads)
            )
        each(n - 1, lambda k: send_sum((i + 1 + k) % n))

        @pl.when(r == 0)
        def _():
            send_sum(i)

    @pl.when(r == 0)
    def _():
        drain(slots.at[pl.ds(0, m - 1)], p_recv)
        mine.wait()
        total_of(slots, m, reduced, 16)
        size = back.shape[0]

        def place(j):
            return back.at[:, pl.ds(pl.multiple_of((j % q) * full, full), full)]

        def block(k):
            return reduced.at[pl.ds(pl.multiple_of(k * size, size), size)]

        def send_block(k):
            @pl.when(t * q + k != i)
            def _():
                remote(block(k), place(i), b_send, b_recv, 0, t * q + k, home).start()

        each(q, send_block)

        @pl.when(home == t)
        def _():
            keep = pltpu.make_async_copy(block(i % q), place(i), loc.at[0])
            keep.start()
            keep.wait()
            if q > 1:
                drain(reduced.at[pl.ds(0, (q - 1) * size)], b_recv)
                drain(reduced.at[pl.ds(0, (q - 1) * size)], b_send)

        @pl.when(home != t)
        def _():
            drain(reduced, b_recv)
            drain(reduced, b_send)

        drain(slots.at[pl.ds(0, m - 1)], p_send)
        if split:
            drain(val_slots.at[pl.ds(0, n)], v_send)

    @pl.when(r == 1)
    def _():
        kept = pltpu.make_async_copy(sums.at[i], val_slots.at[n + i if split else i], loc.at[0])
        kept.start()
        drain(val_slots.at[pl.ds(0, sources - 1)], v_recv)
        kept.wait()
        total_of(val_slots, sources, vals, 16)
        drain(val_slots.at[pl.ds(0, n - 1)], v_send)

    @pl.when(active)
    def _():
        for which in range(2):
            for step in range(1, pairs):
                over(which, step).wait_send()
            for src in range(pairs):
                to_pair(which, src).wait_send()

    for role in targets:
        @pl.when(r != role)
        def _(role=role):
            drain(slabs.at[role, t], hid_send.at[role])

        @pl.when(r == role)
        def _(role=role):
            drain(slabs.at[role, t, pl.ds(0, n - 1)], hid_send.at[role])

    drain(ogs.at[pl.ds(0, n - 1)], og_send)


def fused(hid, og, master, moment1, moment2, n, m):
    q = n // m
    full, heads = master.shape
    tokens = og.shape[0]
    split = full % 256 == 0
    width = full // 2 if split else full
    dma = pltpu.SemaphoreType.DMA
    anywhere = pl.BlockSpec(memory_space=pl.ANY)
    half = pltpu.VMEM((width, heads), jnp.float32)
    block = pltpu.VMEM((m, q * tokens, full), jnp.bfloat16)
    return pl.pallas_call(
        functools.partial(fused_kernel, n, m, split),
        out_shape=(
            jax.ShapeDtypeStruct((tokens, q * full), jnp.bfloat16),
            jax.ShapeDtypeStruct((tokens, heads), jnp.bfloat16),
        ),
        in_specs=[anywhere] * 5,
        out_specs=(anywhere, pl.BlockSpec(memory_space=pltpu.VMEM)),
        scratch_shapes=[
            pltpu.VMEM((2, m, n, tokens // m, width), jnp.bfloat16),
            pltpu.VMEM((n, tokens, heads), jnp.bfloat16),
            pltpu.VMEM((full, heads), jnp.float32),
            half,
            half,
            pltpu.VMEM((width, heads), jnp.bfloat16),
            pltpu.VMEM((n, tokens, heads), jnp.bfloat16),
            block,
            block,
            pltpu.VMEM((q * tokens, full), jnp.bfloat16),
            pltpu.VMEM((n * (2 if split else 1), tokens, heads), jnp.bfloat16),
            dma, dma, dma((2,)), dma((2,)), dma((5,)),
            dma((2, m // 2)), dma((2, m // 2)), dma((2, m // 2)), dma((2, m // 2)),
            dma, dma, dma, dma, dma, dma,
        ],
        compiler_params=pltpu.CompilerParams(
            collective_id=0, has_side_effects=True, vmem_limit_bytes=40 * 2**20
        ),
    )(hid, og, master, moment1, moment2)


def local(
    hidden, out_grad, master, moment1, moment2, queries, new_keys, k_cache, v_cache, cache_len
):
    is_learner = lax.axis_index("role") == 0
    n, m = lax.axis_size("dp"), lax.axis_size("tp")
    learner_rows, values = fused(hidden[0], out_grad, master, moment1, moment2, n, m)
    result = lax.cond(
        is_learner,
        lambda: learner_rows,
        lambda: attend(values, queries, new_keys, k_cache, v_cache, cache_len),
    )
    return result[None]


def attend(values, queries, new_keys, k_cache, v_cache, cache_len):
    heads_here = values.shape[1] // HD
    share = QH // KVH
    replica_rows = cache_len.shape[0]
    cache_size = k_cache.shape[1]
    values = values.reshape(STEPS, replica_rows, heads_here, HD)
    query_all = queries.reshape(STEPS, replica_rows, heads_here, share, HD)
    newkey_all = new_keys.reshape(STEPS, replica_rows, heads_here, HD)
    cache_keys = k_cache.reshape(replica_rows, cache_size, heads_here, HD)
    cache_vals = v_cache.reshape(replica_rows, cache_size, heads_here, HD)
    scale = HD ** (-0.5)
    cache_score = (
        jnp.einsum("srkgd,rpkd->srkgp", query_all, cache_keys, preferred_element_type=jnp.float32)
        * scale
    )
    valid = jnp.arange(cache_size)[None, :] < cache_len[:, None]
    cache_score = jnp.where(valid[None, :, None, None, :], cache_score, neg_fill)
    fresh_score = (
        jnp.einsum("srkgd,trkd->srkgt", query_all, newkey_all, preferred_element_type=jnp.float32)
        * scale
    )
    causal = jnp.arange(STEPS)[:, None] >= jnp.arange(STEPS)[None, :]
    fresh_score = jnp.where(causal[:, None, None, None, :], fresh_score, neg_fill)
    top = jnp.maximum(jnp.max(cache_score, axis=-1), jnp.max(fresh_score, axis=-1))
    cache_exp = jnp.exp(cache_score - top[..., None])
    fresh_exp = jnp.exp(fresh_score - top[..., None])
    total = jnp.sum(cache_exp, axis=-1) + jnp.sum(fresh_exp, axis=-1)
    cache_wts = (cache_exp / total[..., None]).astype(jnp.bfloat16)
    fresh_wts = (fresh_exp / total[..., None]).astype(jnp.bfloat16)
    output = jnp.einsum(
        "srkgp,rpkd->srkgd", cache_wts, cache_vals, preferred_element_type=jnp.float32
    )
    output = output + jnp.einsum(
        "srkgt,trkd->srkgd", fresh_wts, values, preferred_element_type=jnp.float32
    )
    return output.astype(jnp.bfloat16).reshape(STEPS * replica_rows, heads_here * share * HD)


def solution(mesh):
    return jax.shard_map(
        local,
        mesh=mesh,
        in_specs=(
            P("role", "dp", None),
            P("dp", "tp"),
            P("dp", "tp"),
            P("dp", "tp"),
            P("dp", "tp"),
            P(None, "dp", "tp"),
            P(None, "dp", "tp"),
            P("dp", None, "tp"),
            P("dp", None, "tp"),
            P("dp"),
        ),
        out_specs=P("role", "dp", "tp"),
        check_vma=False,
    )
```

```python
import functools

import jax
import jax.numpy as jnp
from jax import lax
from jax.experimental import pallas as pl
from jax.experimental.pallas import tpu as pltpu
from jax.sharding import PartitionSpec as P

D = 8192
KVH = 8
QH = 64
HD = 128
STEPS = 8


beta_one = 0.9
beta_two = 0.95
adam_eps = 1e-08
bias_one = 1.0 - 0.9**10
bias_two = 1.0 - 0.95**10
neg_fill = -1e30


def adam_fresh(master, moment1, moment2, gradient):
    step_size = 2.0 * D ** (-0.5)
    first = beta_one * moment1 + (1.0 - beta_one) * gradient
    second = beta_two * moment2 + (1.0 - beta_two) * gradient * gradient
    change = first / bias_one / (jnp.sqrt(second / bias_two) + adam_eps)
    return (master - step_size * change).astype(jnp.bfloat16)


MESH = pl.DeviceIdType.MESH


def position():
    return lax.axis_index("role"), lax.axis_index("dp"), lax.axis_index("tp")


def signal(semaphore, role, row, col):
    pl.semaphore_signal(semaphore, inc=1, device_id=(role, row, col), device_id_type=MESH)


def remote(src, dst, send, recv, role, row, col):
    return pltpu.make_async_remote_copy(
        src_ref=src,
        dst_ref=dst,
        send_sem=send,
        recv_sem=recv,
        device_id=(role, row, col),
        device_id_type=MESH,
    )


def drain(ref, semaphore):
    pltpu.make_async_copy(ref, ref, semaphore).wait()


def each(count, body):
    def step(k, carry):
        body(k)
        return carry

    lax.fori_loop(0, count, step, 0)


def total_of(slots, count, out, tile):
    def chunk(k):
        at = pl.ds(pl.multiple_of(k * tile, tile), tile)
        total = slots[0, at, :].astype(jnp.float32)
        for s in range(1, count):
            total = total + slots[s, at, :].astype(jnp.float32)
        out[at, :] = total.astype(out.dtype)

    each(out.shape[0] // tile, chunk)


def fused_kernel(
    n, m, split, hid, og, master, moment1, moment2, queries, keys, k_cache, v_cache, lens, back, att,
    slabs, ogs, master_v, moment1_v, moment2_v, fresh, sums, parts, slots, reduced, val_slots,
    og_send, og_recv, hid_send, hid_recv, loc, x_send, x_recv, c_send, c_recv,
    p_send, p_recv, b_send, b_recv, v_send, v_recv,
    vals, queries_v, keys_v, k_v, v_v, cache_out, fresh_wts, att_sem,
):
    r, i, t = position()
    q = n // m
    rows, width = slabs.shape[3], slabs.shape[4]
    full = master.shape[0]
    heads = og.shape[1]
    home = i // q
    pairs = m // 2
    px, core = t // 2, t % 2
    sources = val_slots.shape[0]
    active = (r == 1) | split

    loads = [pltpu.make_async_copy(master, master_v, loc.at[2])]
    first = pl.multiple_of((r * width) if split else 0, width)
    for k, (src, dst) in enumerate(((moment1, moment1_v), (moment2, moment2_v))):
        loads.append(pltpu.make_async_copy(src.at[pl.ds(first, width)], dst, loc.at[3 + k]))
    for load in loads:
        load.start()

    att_loads = [
        pltpu.make_async_copy(src, dst, att_sem.at[k])
        for k, (src, dst) in enumerate(
            ((queries, queries_v), (keys, keys_v), (k_cache, k_v), (v_cache, v_v))
        )
    ]

    @pl.when(r == 1)
    def _():
        for load in att_loads:
            load.start()

    barrier = pltpu.get_barrier_semaphore()

    def greet(k):
        @pl.when(k != r * n + i)
        def _():
            signal(barrier, k // n, k % n, t)

    def greet_tp(k):
        signal(barrier, r, i, (t + 1 + k) % m)

    def greet_far(k):
        @pl.when(t * q + k != i)
        def _():
            signal(barrier, 0, t * q + k, home)

    each(2 * n, greet)
    each(m - 1, greet_tp)

    @pl.when(r == 0)
    def _():
        each(q, greet_far)
        pl.semaphore_wait(barrier, 2 * n - 1 + m - 1 + q - jnp.where(home == t, 1, 0))

    @pl.when(r == 1)
    def _():
        pl.semaphore_wait(barrier, 2 * n - 1 + m - 1)

    def piece(role, j):
        start = j * full + (role * width if split else 0)
        return hid.at[pl.ds(pl.multiple_of(t * rows, rows), rows), pl.ds(pl.multiple_of(start, width), width)]

    def send_og(k):
        j = (i + k) % n
        remote(og, ogs.at[i], og_send, og_recv, r, j, t).start()

    def send_hid(role, j):
        remote(piece(role, j), slabs.at[r, t, i], hid_send.at[role], hid_recv.at[r], role, j, t).start()

    each(n - 1, lambda k: send_og(k + 1))
    targets = (0, 1) if split else (1,)
    for role in targets:
        each(n - 1, lambda k, role=role: send_hid(role, (i + k + 1) % n))

        @pl.when(r != role)
        def _(role=role):
            send_hid(role, i)

    og_local = pltpu.make_async_copy(og, ogs.at[i], loc.at[0])
    og_local.start()

    replica_rows, kv_heads, asked = queries.shape[:3]
    half_rows = replica_rows // 2

    def attend_row(row):
        for k in range(kv_heads):
            at = slice(k * HD, (k + 1) * HD)
            cache_score, fresh_score = [
                lax.dot_general(
                    queries_v[row, k], known, (((1,), (1,)), ((), ())), preferred_element_type=jnp.float32
                )
                * HD ** (-0.5)
                for known in (k_v[row, :, at], keys_v[:, at])
            ]
            place = lax.broadcasted_iota(jnp.int32, cache_score.shape, 1)
            cache_score = jnp.where(place < lens[row], cache_score, neg_fill)
            token = lax.broadcasted_iota(jnp.int32, fresh_score.shape, 1)
            step = lax.broadcasted_iota(jnp.int32, fresh_score.shape, 0) // (asked // STEPS)
            seen = (token % replica_rows == row) & (token // replica_rows <= step)
            fresh_score = jnp.where(seen, fresh_score, neg_fill)
            top = jnp.maximum(
                jnp.max(cache_score, axis=-1, keepdims=True), jnp.max(fresh_score, axis=-1, keepdims=True)
            )
            cache_exp = jnp.exp(cache_score - top)
            fresh_exp = jnp.exp(fresh_score - top)
            total = jnp.sum(cache_exp, axis=-1, keepdims=True) + jnp.sum(fresh_exp, axis=-1, keepdims=True)
            cache_wts = (cache_exp / total).astype(jnp.bfloat16)
            fresh_wts[row, k] = (fresh_exp / total).astype(jnp.bfloat16)
            cache_out[row, k] = jnp.dot(cache_wts, v_v[row, :, at], preferred_element_type=jnp.float32)

    def finish_row(row):
        for k in range(kv_heads):
            new = jnp.dot(
                fresh_wts[row, k], vals[:, k * HD : (k + 1) * HD], preferred_element_type=jnp.float32
            )
            att[row, k] = (cache_out[row, k] + new).astype(att.dtype)

    @pl.when(r == 1)
    def _():
        for load in att_loads:
            load.wait()
        each(half_rows, attend_row)

    def to_pair(which, src):
        return remote(
            slabs.at[which, src * 2 + core],
            slabs.at[which, src * 2 + core],
            c_send.at[which, src],
            c_recv.at[which, src],
            r, i, t + 1 - 2 * core,
        )

    def from_pair(which, src):
        drain(slabs.at[which, src * 2 + 1 - core], c_recv.at[which, src])

    def over(which, step):
        dst = (px + step) % pairs
        return remote(
            slabs.at[which, t],
            slabs.at[which, t],
            x_send.at[which, step],
            x_recv.at[which, px],
            r, i, dst * 2 + core,
        )

    @pl.when(active)
    def _():
        own = pltpu.make_async_copy(piece(r, i), slabs.at[r, t, i], loc.at[1])
        own.start()
        for which in range(2):
            @pl.when(r != which)
            def _(which=which):
                drain(slabs.at[which, t], hid_recv.at[which])

            @pl.when(r == which)
            def _(which=which):
                drain(slabs.at[which, t, pl.ds(0, n - 1)], hid_recv.at[which])
                own.wait()

            for step in range(1, pairs):
                over(which, step).start()
            to_pair(which, px).start()

    drain(ogs.at[pl.ds(0, n - 1)], og_recv)
    og_local.wait()
    for load in loads:
        load.wait()

    @pl.when(r == 1)
    def _():
        each(replica_rows - half_rows, lambda k: attend_row(half_rows + k))

    chunk = min(512, full)
    block_rows = q * og.shape[0]

    def fill_part(g):
        tokens = ogs[pl.ds(g * q, q)].reshape(block_rows, heads)

        def columns(k):
            at = pl.ds(pl.multiple_of(k * chunk, chunk), chunk)
            parts[g, :, at] = lax.dot_general(
                tokens,
                master_v[at, :].astype(jnp.bfloat16),
                (((1,), (1,)), ((), ())),
                preferred_element_type=jnp.float32,
            ).astype(jnp.bfloat16)

        each(full // chunk, columns)

    mine = pltpu.make_async_copy(parts.at[t], slots.at[t], loc.at[0])

    @pl.when(r == 0)
    def _():
        def send_part(k):
            g = (t + 1 + k) % m
            fill_part(g)
            remote(parts.at[g], slots.at[t], p_send, p_recv, 0, i, g).start()

        each(m - 1, send_part)
        fill_part(t)
        mine.start()

    def send_sum(j):
        slot = r * n + i if split else i
        remote(sums.at[j], val_slots.at[slot], v_send, v_recv, 1, j, t).start()

    @pl.when(active)
    def _():
        for which in range(2):
            for step in range(1, pairs):
                src = (px + step) % pairs
                drain(slabs.at[which, src * 2 + core], x_recv.at[which, src])
                to_pair(which, src).start()
        for src in range(pairs):
            from_pair(0, src)

        tile = min(256, width)

        def update(k):
            at = pl.ds(pl.multiple_of(k * tile, tile), tile)
            gradient = jnp.zeros((tile, heads), jnp.float32)
            for g in range(m):
                gradient = gradient + lax.dot_general(
                    slabs[0, g, :, :, at].reshape(n * rows, tile),
                    ogs[:, g * rows : (g + 1) * rows, :].reshape(n * rows, heads),
                    (((0,), (0,)), ((), ())),
                    preferred_element_type=jnp.float32,
                )
            held = pl.ds(pl.multiple_of(first + k * tile, tile), tile)
            fresh[at, :] = adam_fresh(master_v[held, :], moment1_v[at, :], moment2_v[at, :], gradient)

        each(width // tile, update)
        for src in range(pairs):
            from_pair(1, src)
        for g in range(m):
            sums[:, g * rows : (g + 1) * rows, :] = (
                jnp.dot(
                    slabs[1, g].reshape(n * rows, width), fresh[...], preferred_element_type=jnp.float32
                )
                .astype(jnp.bfloat16)
                .reshape(n, rows, heads)
            )
        each(n - 1, lambda k: send_sum((i + 1 + k) % n))

        @pl.when(r == 0)
        def _():
            send_sum(i)

    @pl.when(r == 0)
    def _():
        drain(slots.at[pl.ds(0, m - 1)], p_recv)
        mine.wait()
        total_of(slots, m, reduced, 16)
        size = back.shape[0]

        def place(j):
            return back.at[:, pl.ds(pl.multiple_of((j % q) * full, full), full)]

        def block(k):
            return reduced.at[pl.ds(pl.multiple_of(k * size, size), size)]

        def send_block(k):
            @pl.when(t * q + k != i)
            def _():
                remote(block(k), place(i), b_send, b_recv, 0, t * q + k, home).start()

        each(q, send_block)

        @pl.when(home == t)
        def _():
            keep = pltpu.make_async_copy(block(i % q), place(i), loc.at[0])
            keep.start()
            keep.wait()
            if q > 1:
                drain(reduced.at[pl.ds(0, (q - 1) * size)], b_recv)
                drain(reduced.at[pl.ds(0, (q - 1) * size)], b_send)

        @pl.when(home != t)
        def _():
            drain(reduced, b_recv)
            drain(reduced, b_send)

        drain(slots.at[pl.ds(0, m - 1)], p_send)
        if split:
            drain(val_slots.at[pl.ds(0, n)], v_send)

    @pl.when(r == 1)
    def _():
        kept = pltpu.make_async_copy(sums.at[i], val_slots.at[n + i if split else i], loc.at[0])
        kept.start()
        drain(val_slots.at[pl.ds(0, sources - 1)], v_recv)
        kept.wait()
        total_of(val_slots, sources, vals, 16)
        each(replica_rows, finish_row)
        drain(val_slots.at[pl.ds(0, n - 1)], v_send)

    @pl.when(active)
    def _():
        for which in range(2):
            for step in range(1, pairs):
                over(which, step).wait_send()
            for src in range(pairs):
                to_pair(which, src).wait_send()

    for role in targets:
        @pl.when(r != role)
        def _(role=role):
            drain(slabs.at[role, t], hid_send.at[role])

        @pl.when(r == role)
        def _(role=role):
            drain(slabs.at[role, t, pl.ds(0, n - 1)], hid_send.at[role])

    drain(ogs.at[pl.ds(0, n - 1)], og_send)


def fused(hid, og, master, moment1, moment2, queries, keys, k_cache, v_cache, lens, n, m):
    q = n // m
    full, heads = master.shape
    tokens = og.shape[0]
    split = full % 256 == 0
    width = full // 2 if split else full
    dma = pltpu.SemaphoreType.DMA
    anywhere = pl.BlockSpec(memory_space=pltpu.HBM)
    half = pltpu.VMEM((width, heads), jnp.float32)
    block = pltpu.VMEM((m, q * tokens, full), jnp.bfloat16)
    return pl.pallas_call(
        functools.partial(fused_kernel, n, m, split),
        out_shape=(
            jax.ShapeDtypeStruct((tokens, q * full), jnp.bfloat16),
            jax.ShapeDtypeStruct(queries.shape, jnp.bfloat16),
        ),
        in_specs=[anywhere] * 9 + [pl.BlockSpec(memory_space=pltpu.SMEM)],
        out_specs=(anywhere, pl.BlockSpec(memory_space=pltpu.VMEM)),
        scratch_shapes=[
            pltpu.VMEM((2, m, n, tokens // m, width), jnp.bfloat16),
            pltpu.VMEM((n, tokens, heads), jnp.bfloat16),
            pltpu.VMEM((full, heads), jnp.float32),
            half,
            half,
            pltpu.VMEM((width, heads), jnp.bfloat16),
            pltpu.VMEM((n, tokens, heads), jnp.bfloat16),
            block,
            block,
            pltpu.VMEM((q * tokens, full), jnp.bfloat16),
            pltpu.VMEM((n * (2 if split else 1), tokens, heads), jnp.bfloat16),
            dma, dma, dma((2,)), dma((2,)), dma((5,)),
            dma((2, m // 2)), dma((2, m // 2)), dma((2, m // 2)), dma((2, m // 2)),
            dma, dma, dma, dma, dma, dma,
            pltpu.VMEM((tokens, heads), jnp.bfloat16),
            pltpu.VMEM(queries.shape, queries.dtype),
            pltpu.VMEM(keys.shape, keys.dtype),
            pltpu.VMEM(k_cache.shape, k_cache.dtype),
            pltpu.VMEM(v_cache.shape, v_cache.dtype),
            pltpu.VMEM(queries.shape, jnp.float32),
            pltpu.VMEM(queries.shape[:3] + (tokens,), jnp.bfloat16),
            dma((4,)),
        ],
        compiler_params=pltpu.CompilerParams(
            collective_id=0, has_side_effects=True, vmem_limit_bytes=60 * 2**20
        ),
    )(hid, og, master, moment1, moment2, queries, keys, k_cache, v_cache, lens)


def local(
    hidden, out_grad, master, moment1, moment2, queries, new_keys, k_cache, v_cache, cache_len
):
    is_learner = lax.axis_index("role") == 0
    n, m = lax.axis_size("dp"), lax.axis_size("tp")
    replica_rows = cache_len.shape[0]
    heads_here = out_grad.shape[1] // HD
    share = QH // KVH
    asked = queries.reshape(STEPS, replica_rows, heads_here, share, HD).transpose(1, 2, 0, 3, 4)
    learner_rows, attended = fused(
        hidden[0],
        out_grad,
        master,
        moment1,
        moment2,
        asked.reshape(replica_rows, heads_here, STEPS * share, HD),
        new_keys.reshape(STEPS * replica_rows, heads_here * HD),
        k_cache,
        v_cache,
        cache_len,
        n,
        m,
    )
    decoded = attended.reshape(replica_rows, heads_here, STEPS, share, HD).transpose(2, 0, 1, 3, 4)
    result = jnp.where(is_learner, learner_rows, decoded.reshape(learner_rows.shape))
    return result[None]


def solution(mesh):
    return jax.shard_map(
        local,
        mesh=mesh,
        in_specs=(
            P("role", "dp", None),
            P("dp", "tp"),
            P("dp", "tp"),
            P("dp", "tp"),
            P("dp", "tp"),
            P(None, "dp", "tp"),
            P(None, "dp", "tp"),
            P("dp", None, "tp"),
            P("dp", None, "tp"),
            P("dp"),
        ),
        out_specs=P("role", "dp", "tp"),
        check_vma=False,
    )
```

```python
import functools

import jax
import jax.numpy as jnp
from jax import lax
from jax.experimental import pallas as pl
from jax.experimental.pallas import tpu as pltpu
from jax.sharding import PartitionSpec as P

D = 8192
KVH = 8
QH = 64
HD = 128
STEPS = 8


beta_one = 0.9
beta_two = 0.95
adam_eps = 1e-08
bias_one = 1.0 - 0.9**10
bias_two = 1.0 - 0.95**10
neg_fill = -1e30


def adam_fresh(master, moment1, moment2, gradient):
    step_size = 2.0 * D ** (-0.5)
    first = beta_one * moment1 + (1.0 - beta_one) * gradient
    second = beta_two * moment2 + (1.0 - beta_two) * gradient * gradient
    change = first / bias_one / (jnp.sqrt(second / bias_two) + adam_eps)
    return (master - step_size * change).astype(jnp.bfloat16)


MESH = pl.DeviceIdType.MESH


def position():
    return lax.axis_index("role"), lax.axis_index("dp"), lax.axis_index("tp")


def signal(semaphore, role, row, col):
    pl.semaphore_signal(semaphore, inc=1, device_id=(role, row, col), device_id_type=MESH)


def remote(src, dst, send, recv, role, row, col):
    return pltpu.make_async_remote_copy(
        src_ref=src,
        dst_ref=dst,
        send_sem=send,
        recv_sem=recv,
        device_id=(role, row, col),
        device_id_type=MESH,
    )


def drain(ref, semaphore):
    pltpu.make_async_copy(ref, ref, semaphore).wait()


def each(count, body):
    def step(k, carry):
        body(k)
        return carry

    lax.fori_loop(0, count, step, 0)


def total_of(slots, count, out, tile):
    def chunk(k):
        at = pl.ds(pl.multiple_of(k * tile, tile), tile)
        total = slots[0, at, :].astype(jnp.float32)
        for s in range(1, count):
            total = total + slots[s, at, :].astype(jnp.float32)
        out[at, :] = total.astype(out.dtype)

    each(out.shape[0] // tile, chunk)


def fused_kernel(
    n, m, split, hid, og, master, moment1, moment2, queries, keys, k_cache, v_cache, lens, back, att,
    slabs, ogs, master_v, moment1_v, moment2_v, fresh, sums, parts, slots, reduced, val_slots,
    og_send, og_recv, hid_send, hid_recv, loc, x_send, x_recv, c_send, c_recv,
    p_send, p_recv, b_send, b_recv, v_send, v_recv,
    vals, queries_v, keys_v, k_v, v_v, cache_out, fresh_wts, att_sem,
):
    r, i, t = position()
    q = n // m
    rows, width = slabs.shape[3], slabs.shape[4]
    full = master.shape[0]
    heads = og.shape[1]
    home = i // q
    pairs = m // 2
    px, core = t // 2, t % 2
    sources = val_slots.shape[0]
    active = (r == 1) | split

    loads = [pltpu.make_async_copy(master, master_v, loc.at[2])]
    first = pl.multiple_of((r * width) if split else 0, width)
    for k, (src, dst) in enumerate(((moment1, moment1_v), (moment2, moment2_v))):
        loads.append(pltpu.make_async_copy(src.at[pl.ds(first, width)], dst, loc.at[3 + k]))
    for load in loads:
        load.start()

    att_loads = [
        pltpu.make_async_copy(src, dst, att_sem.at[k])
        for k, (src, dst) in enumerate(
            ((queries, queries_v), (keys, keys_v), (k_cache, k_v), (v_cache, v_v))
        )
    ]

    @pl.when(r == 1)
    def _():
        for load in att_loads:
            load.start()

    barrier = pltpu.get_barrier_semaphore()

    def greet(k):
        @pl.when(k != r * n + i)
        def _():
            signal(barrier, k // n, k % n, t)

    def greet_tp(k):
        signal(barrier, r, i, (t + 1 + k) % m)

    def greet_far(k):
        @pl.when(t * q + k != i)
        def _():
            signal(barrier, 0, t * q + k, home)

        signal(barrier, 1, t * q + k, home)

    each(2 * n, greet)
    each(m - 1, greet_tp)

    @pl.when(r == 0)
    def _():
        each(q, greet_far)
        pl.semaphore_wait(barrier, 2 * n - 1 + m - 1 + q - jnp.where(home == t, 1, 0))

    @pl.when(r == 1)
    def _():
        pl.semaphore_wait(barrier, 2 * n - 1 + m - 1 + q)

    def piece(role, j):
        start = j * full + (role * width if split else 0)
        return hid.at[pl.ds(pl.multiple_of(t * rows, rows), rows), pl.ds(pl.multiple_of(start, width), width)]

    def send_og(k):
        j = (i + k) % n
        remote(og, ogs.at[i], og_send, og_recv, r, j, t).start()

    def send_hid(role, j):
        remote(piece(role, j), slabs.at[r, t, i], hid_send.at[role], hid_recv.at[r], role, j, t).start()

    each(n - 1, lambda k: send_og(k + 1))
    targets = (0, 1) if split else (1,)
    for role in targets:
        each(n - 1, lambda k, role=role: send_hid(role, (i + k + 1) % n))

        @pl.when(r != role)
        def _(role=role):
            send_hid(role, i)

    og_local = pltpu.make_async_copy(og, ogs.at[i], loc.at[0])
    og_local.start()

    replica_rows, kv_heads, asked = queries.shape[:3]
    half_rows = replica_rows // 2

    def attend_row(row):
        for k in range(kv_heads):
            at = slice(k * HD, (k + 1) * HD)
            cache_score, fresh_score = [
                lax.dot_general(
                    queries_v[row, k], known, (((1,), (1,)), ((), ())), preferred_element_type=jnp.float32
                )
                * HD ** (-0.5)
                for known in (k_v[row, :, at], keys_v[:, at])
            ]
            place = lax.broadcasted_iota(jnp.int32, cache_score.shape, 1)
            cache_score = jnp.where(place < lens[row], cache_score, neg_fill)
            token = lax.broadcasted_iota(jnp.int32, fresh_score.shape, 1)
            step = lax.broadcasted_iota(jnp.int32, fresh_score.shape, 0) // (asked // STEPS)
            seen = (token % replica_rows == row) & (token // replica_rows <= step)
            fresh_score = jnp.where(seen, fresh_score, neg_fill)
            top = jnp.maximum(
                jnp.max(cache_score, axis=-1, keepdims=True), jnp.max(fresh_score, axis=-1, keepdims=True)
            )
            cache_exp = jnp.exp(cache_score - top)
            fresh_exp = jnp.exp(fresh_score - top)
            total = jnp.sum(cache_exp, axis=-1, keepdims=True) + jnp.sum(fresh_exp, axis=-1, keepdims=True)
            cache_wts = (cache_exp / total).astype(jnp.bfloat16)
            fresh_wts[row, k] = (fresh_exp / total).astype(jnp.bfloat16)
            cache_out[row, k] = jnp.dot(cache_wts, v_v[row, :, at], preferred_element_type=jnp.float32)

    def finish_row(row):
        for k in range(kv_heads):
            new = jnp.dot(
                fresh_wts[row, k], vals[:, k * HD : (k + 1) * HD], preferred_element_type=jnp.float32
            )
            att[row, k] = (cache_out[row, k] + new).astype(att.dtype)

    @pl.when(r == 1)
    def _():
        for load in att_loads:
            load.wait()
        each(half_rows, attend_row)

    def to_pair(which, src):
        return remote(
            slabs.at[which, src * 2 + core],
            slabs.at[which, src * 2 + core],
            c_send.at[which, src],
            c_recv.at[which, src],
            r, i, t + 1 - 2 * core,
        )

    def from_pair(which, src):
        drain(slabs.at[which, src * 2 + 1 - core], c_recv.at[which, src])

    def over(which, step):
        dst = (px + step) % pairs
        return remote(
            slabs.at[which, t],
            slabs.at[which, t],
            x_send.at[which, step],
            x_recv.at[which, px],
            r, i, dst * 2 + core,
        )

    @pl.when(active)
    def _():
        own = pltpu.make_async_copy(piece(r, i), slabs.at[r, t, i], loc.at[1])
        own.start()
        for which in range(2):
            @pl.when(r != which)
            def _(which=which):
                drain(slabs.at[which, t], hid_recv.at[which])

            @pl.when(r == which)
            def _(which=which):
                drain(slabs.at[which, t, pl.ds(0, n - 1)], hid_recv.at[which])
                own.wait()

            for step in range(1, pairs):
                over(which, step).start()
            to_pair(which, px).start()

    drain(ogs.at[pl.ds(0, n - 1)], og_recv)
    og_local.wait()
    for load in loads:
        load.wait()

    chunk = min(512, full)
    part_rows = og.shape[0] // 2
    block_rows = q * part_rows
    own_half = pl.ds(pl.multiple_of(r * part_rows, part_rows), part_rows)

    def fill_part(g):
        tokens = ogs[pl.ds(g * q, q), own_half, :].reshape(block_rows, heads)

        def columns(k):
            at = pl.ds(pl.multiple_of(k * chunk, chunk), chunk)
            parts[g, :, at] = lax.dot_general(
                tokens,
                master_v[at, :].astype(jnp.bfloat16),
                (((1,), (1,)), ((), ())),
                preferred_element_type=jnp.float32,
            ).astype(jnp.bfloat16)

        each(full // chunk, columns)

    mine = pltpu.make_async_copy(parts.at[t], slots.at[t], loc.at[0])

    def send_part(k):
        g = (t + 1 + k) % m
        fill_part(g)
        remote(parts.at[g], slots.at[t], p_send, p_recv, r, i, g).start()

    each(m - 1, send_part)
    fill_part(t)
    mine.start()

    @pl.when(r == 1)
    def _():
        each(replica_rows - half_rows, lambda k: attend_row(half_rows + k))

    def send_sum(j):
        slot = r * n + i if split else i
        remote(sums.at[j], val_slots.at[slot], v_send, v_recv, 1, j, t).start()

    @pl.when(active)
    def _():
        for which in range(2):
            for step in range(1, pairs):
                src = (px + step) % pairs
                drain(slabs.at[which, src * 2 + core], x_recv.at[which, src])
                to_pair(which, src).start()
        for src in range(pairs):
            from_pair(0, src)

        tile = min(256, width)

        def update(k):
            at = pl.ds(pl.multiple_of(k * tile, tile), tile)
            gradient = jnp.zeros((tile, heads), jnp.float32)
            for g in range(m):
                gradient = gradient + lax.dot_general(
                    slabs[0, g, :, :, at].reshape(n * rows, tile),
                    ogs[:, g * rows : (g + 1) * rows, :].reshape(n * rows, heads),
                    (((0,), (0,)), ((), ())),
                    preferred_element_type=jnp.float32,
                )
            held = pl.ds(pl.multiple_of(first + k * tile, tile), tile)
            fresh[at, :] = adam_fresh(master_v[held, :], moment1_v[at, :], moment2_v[at, :], gradient)

        each(width // tile, update)
        for src in range(pairs):
            from_pair(1, src)
        for g in range(m):
            sums[:, g * rows : (g + 1) * rows, :] = (
                jnp.dot(
                    slabs[1, g].reshape(n * rows, width), fresh[...], preferred_element_type=jnp.float32
                )
                .astype(jnp.bfloat16)
                .reshape(n, rows, heads)
            )
        each(n - 1, lambda k: send_sum((i + 1 + k) % n))

        @pl.when(r == 0)
        def _():
            send_sum(i)

    drain(slots.at[pl.ds(0, m - 1)], p_recv)
    mine.wait()
    total_of(slots, m, reduced, 16)

    def place(j):
        return back.at[own_half, pl.ds(pl.multiple_of((j % q) * full, full), full)]

    def block(k):
        return reduced.at[pl.ds(pl.multiple_of(k * part_rows, part_rows), part_rows)]

    def send_block(k):
        @pl.when((r == 1) | (t * q + k != i))
        def _():
            remote(block(k), place(i), b_send, b_recv, 0, t * q + k, home).start()

    each(q, send_block)

    @pl.when((r == 0) & (home == t))
    def _():
        keep = pltpu.make_async_copy(block(i % q), place(i), loc.at[0])
        keep.start()
        keep.wait()
        drain(reduced, b_recv)
        if q > 1:
            drain(reduced.at[pl.ds(0, (q - 1) * part_rows)], b_recv)
            drain(reduced.at[pl.ds(0, (q - 1) * part_rows)], b_send)

    @pl.when((r == 0) & (home != t))
    def _():
        drain(back, b_recv)
        drain(reduced, b_send)

    @pl.when(r == 0)
    def _():
        if split:
            drain(val_slots.at[pl.ds(0, n)], v_send)

    @pl.when(r == 1)
    def _():
        kept = pltpu.make_async_copy(sums.at[i], val_slots.at[n + i if split else i], loc.at[0])
        kept.start()
        drain(val_slots.at[pl.ds(0, sources - 1)], v_recv)
        kept.wait()
        total_of(val_slots, sources, vals, 16)
        each(replica_rows, finish_row)
        drain(val_slots.at[pl.ds(0, n - 1)], v_send)
        drain(reduced, b_send)

    drain(slots.at[pl.ds(0, m - 1)], p_send)

    @pl.when(active)
    def _():
        for which in range(2):
            for step in range(1, pairs):
                over(which, step).wait_send()
            for src in range(pairs):
                to_pair(which, src).wait_send()

    for role in targets:
        @pl.when(r != role)
        def _(role=role):
            drain(slabs.at[role, t], hid_send.at[role])

        @pl.when(r == role)
        def _(role=role):
            drain(slabs.at[role, t, pl.ds(0, n - 1)], hid_send.at[role])

    drain(ogs.at[pl.ds(0, n - 1)], og_send)


def fused(hid, og, master, moment1, moment2, queries, keys, k_cache, v_cache, lens, n, m):
    q = n // m
    full, heads = master.shape
    tokens = og.shape[0]
    split = full % 256 == 0
    width = full // 2 if split else full
    dma = pltpu.SemaphoreType.DMA
    anywhere = pl.BlockSpec(memory_space=pltpu.HBM)
    half = pltpu.VMEM((width, heads), jnp.float32)
    block = pltpu.VMEM((m, q * (tokens // 2), full), jnp.bfloat16)
    return pl.pallas_call(
        functools.partial(fused_kernel, n, m, split),
        out_shape=(
            jax.ShapeDtypeStruct((tokens, q * full), jnp.bfloat16),
            jax.ShapeDtypeStruct(queries.shape, jnp.bfloat16),
        ),
        in_specs=[anywhere] * 9 + [pl.BlockSpec(memory_space=pltpu.SMEM)],
        out_specs=(anywhere, pl.BlockSpec(memory_space=pltpu.VMEM)),
        scratch_shapes=[
            pltpu.VMEM((2, m, n, tokens // m, width), jnp.bfloat16),
            pltpu.VMEM((n, tokens, heads), jnp.bfloat16),
            pltpu.VMEM((full, heads), jnp.float32),
            half,
            half,
            pltpu.VMEM((width, heads), jnp.bfloat16),
            pltpu.VMEM((n, tokens, heads), jnp.bfloat16),
            block,
            block,
            pltpu.VMEM((q * (tokens // 2), full), jnp.bfloat16),
            pltpu.VMEM((n * (2 if split else 1), tokens, heads), jnp.bfloat16),
            dma, dma, dma((2,)), dma((2,)), dma((5,)),
            dma((2, m // 2)), dma((2, m // 2)), dma((2, m // 2)), dma((2, m // 2)),
            dma, dma, dma, dma, dma, dma,
            pltpu.VMEM((tokens, heads), jnp.bfloat16),
            pltpu.VMEM(queries.shape, queries.dtype),
            pltpu.VMEM(keys.shape, keys.dtype),
            pltpu.VMEM(k_cache.shape, k_cache.dtype),
            pltpu.VMEM(v_cache.shape, v_cache.dtype),
            pltpu.VMEM(queries.shape, jnp.float32),
            pltpu.VMEM(queries.shape[:3] + (tokens,), jnp.bfloat16),
            dma((4,)),
        ],
        compiler_params=pltpu.CompilerParams(
            collective_id=0, has_side_effects=True, vmem_limit_bytes=60 * 2**20
        ),
    )(hid, og, master, moment1, moment2, queries, keys, k_cache, v_cache, lens)


def local(
    hidden, out_grad, master, moment1, moment2, queries, new_keys, k_cache, v_cache, cache_len
):
    is_learner = lax.axis_index("role") == 0
    n, m = lax.axis_size("dp"), lax.axis_size("tp")
    replica_rows = cache_len.shape[0]
    heads_here = out_grad.shape[1] // HD
    share = QH // KVH
    asked = queries.reshape(STEPS, replica_rows, heads_here, share, HD).transpose(1, 2, 0, 3, 4)
    learner_rows, attended = fused(
        hidden[0],
        out_grad,
        master,
        moment1,
        moment2,
        asked.reshape(replica_rows, heads_here, STEPS * share, HD),
        new_keys.reshape(STEPS * replica_rows, heads_here * HD),
        k_cache,
        v_cache,
        cache_len,
        n,
        m,
    )
    decoded = attended.reshape(replica_rows, heads_here, STEPS, share, HD).transpose(2, 0, 1, 3, 4)
    result = jnp.where(is_learner, learner_rows, decoded.reshape(learner_rows.shape))
    return result[None]


def solution(mesh):
    return jax.shard_map(
        local,
        mesh=mesh,
        in_specs=(
            P("role", "dp", None),
            P("dp", "tp"),
            P("dp", "tp"),
            P("dp", "tp"),
            P("dp", "tp"),
            P(None, "dp", "tp"),
            P(None, "dp", "tp"),
            P("dp", None, "tp"),
            P("dp", None, "tp"),
            P("dp"),
        ),
        out_specs=P("role", "dp", "tp"),
        check_vma=False,
    )
```

```python
import functools

import jax
import jax.numpy as jnp
from jax import lax
from jax.experimental import pallas as pl
from jax.experimental.pallas import tpu as pltpu
from jax.sharding import PartitionSpec as P

D = 8192
KVH = 8
QH = 64
HD = 128
STEPS = 8


beta_one = 0.9
beta_two = 0.95
adam_eps = 1e-08
bias_one = 1.0 - 0.9**10
bias_two = 1.0 - 0.95**10
neg_fill = -1e30


def adam_fresh(master, moment1, moment2, gradient):
    step_size = 2.0 * D ** (-0.5)
    first = beta_one * moment1 + (1.0 - beta_one) * gradient
    second = beta_two * moment2 + (1.0 - beta_two) * gradient * gradient
    change = first / bias_one / (jnp.sqrt(second / bias_two) + adam_eps)
    return (master - step_size * change).astype(jnp.bfloat16)


MESH = pl.DeviceIdType.MESH


def position():
    return lax.axis_index("role"), lax.axis_index("dp"), lax.axis_index("tp")


def signal(semaphore, role, row, col):
    pl.semaphore_signal(semaphore, inc=1, device_id=(role, row, col), device_id_type=MESH)


def remote(src, dst, send, recv, role, row, col):
    return pltpu.make_async_remote_copy(
        src_ref=src,
        dst_ref=dst,
        send_sem=send,
        recv_sem=recv,
        device_id=(role, row, col),
        device_id_type=MESH,
    )


def drain(ref, semaphore):
    pltpu.make_async_copy(ref, ref, semaphore).wait()


def each(count, body):
    def step(k, carry):
        body(k)
        return carry

    lax.fori_loop(0, count, step, 0)


def total_of(slots, count, out, tile):
    def chunk(k):
        at = pl.ds(pl.multiple_of(k * tile, tile), tile)
        total = slots[0, at, :].astype(jnp.float32)
        for s in range(1, count):
            total = total + slots[s, at, :].astype(jnp.float32)
        out[at, :] = total.astype(out.dtype)

    each(out.shape[0] // tile, chunk)


def fused_kernel(
    n, m, split, hid, og, master, moment1, moment2, queries, keys, k_cache, v_cache, lens, back, att,
    slabs, ogs, master_v, moment1_v, moment2_v, fresh, sums, parts, slots, reduced, val_slots,
    og_send, og_recv, hid_send, hid_recv, loc, x_send, x_recv, c_send, c_recv,
    p_send, p_recv, b_send, b_recv, v_send, v_recv,
    vals, queries_v, keys_v, k_v, v_v, cache_out, fresh_wts, att_sem,
):
    r, i, t = position()
    q = n // m
    rows, width = slabs.shape[3], slabs.shape[4]
    full = master.shape[0]
    heads = og.shape[1]
    home = i // q
    pairs = m // 2
    px, core = t // 2, t % 2
    sources = val_slots.shape[0]
    active = (r == 1) | split

    loads = [pltpu.make_async_copy(master, master_v, loc.at[2])]
    first = pl.multiple_of((r * width) if split else 0, width)
    for k, (src, dst) in enumerate(((moment1, moment1_v), (moment2, moment2_v))):
        loads.append(pltpu.make_async_copy(src.at[pl.ds(first, width)], dst, loc.at[3 + k]))
    for load in loads:
        load.start()

    att_loads = [
        pltpu.make_async_copy(src, dst, att_sem.at[k])
        for k, (src, dst) in enumerate(
            ((queries, queries_v), (keys, keys_v), (k_cache, k_v), (v_cache, v_v))
        )
    ]

    @pl.when(r == 1)
    def _():
        for load in att_loads:
            load.start()

    barrier = pltpu.get_barrier_semaphore()

    def greet(k):
        @pl.when(k != r * n + i)
        def _():
            signal(barrier, k // n, k % n, t)

    def greet_tp(k):
        signal(barrier, r, i, (t + 1 + k) % m)

    def greet_far(k):
        @pl.when(t * q + k != i)
        def _():
            signal(barrier, 0, t * q + k, home)

        signal(barrier, 1, t * q + k, home)

    each(2 * n, greet)
    each(m - 1, greet_tp)

    @pl.when(r == 0)
    def _():
        each(q, greet_far)
        pl.semaphore_wait(barrier, 2 * n - 1 + m - 1 + q - jnp.where(home == t, 1, 0))

    @pl.when(r == 1)
    def _():
        pl.semaphore_wait(barrier, 2 * n - 1 + m - 1 + q)

    def piece(role, j):
        start = j * full + (role * width if split else 0)
        return hid.at[pl.ds(pl.multiple_of(t * rows, rows), rows), pl.ds(pl.multiple_of(start, width), width)]

    def send_og(k):
        j = (i + k) % n
        remote(og, ogs.at[i], og_send, og_recv, r, j, t).start()

    def send_hid(role, j):
        remote(piece(role, j), slabs.at[r, t, i], hid_send.at[role], hid_recv.at[r], role, j, t).start()

    each(n - 1, lambda k: send_og(k + 1))
    targets = (0, 1) if split else (1,)
    for role in targets:
        each(n - 1, lambda k, role=role: send_hid(role, (i + k + 1) % n))

        @pl.when(r != role)
        def _(role=role):
            send_hid(role, i)

    og_local = pltpu.make_async_copy(og, ogs.at[i], loc.at[0])
    og_local.start()

    replica_rows, kv_heads, asked = queries.shape[:3]
    half_rows = replica_rows // 2

    def attend_row(row):
        for k in range(kv_heads):
            at = slice(k * HD, (k + 1) * HD)
            cache_score, fresh_score = [
                lax.dot_general(
                    queries_v[row, k], known, (((1,), (1,)), ((), ())), preferred_element_type=jnp.float32
                )
                * HD ** (-0.5)
                for known in (k_v[row, :, at], keys_v[:, at])
            ]
            place = lax.broadcasted_iota(jnp.int32, cache_score.shape, 1)
            cache_score = jnp.where(place < lens[row], cache_score, neg_fill)
            token = lax.broadcasted_iota(jnp.int32, fresh_score.shape, 1)
            step = lax.broadcasted_iota(jnp.int32, fresh_score.shape, 0) // (asked // STEPS)
            seen = (token % replica_rows == row) & (token // replica_rows <= step)
            fresh_score = jnp.where(seen, fresh_score, neg_fill)
            top = jnp.maximum(
                jnp.max(cache_score, axis=-1, keepdims=True), jnp.max(fresh_score, axis=-1, keepdims=True)
            )
            cache_exp = jnp.exp(cache_score - top)
            fresh_exp = jnp.exp(fresh_score - top)
            total = jnp.sum(cache_exp, axis=-1, keepdims=True) + jnp.sum(fresh_exp, axis=-1, keepdims=True)
            cache_wts = (cache_exp / total).astype(jnp.bfloat16)
            fresh_wts[row, k] = (fresh_exp / total).astype(jnp.bfloat16)
            cache_out[row, k] = jnp.dot(cache_wts, v_v[row, :, at], preferred_element_type=jnp.float32)

    def finish_row(row):
        for k in range(kv_heads):
            new = jnp.dot(
                fresh_wts[row, k], vals[:, k * HD : (k + 1) * HD], preferred_element_type=jnp.float32
            )
            att[row, k] = (cache_out[row, k] + new).astype(att.dtype)

    @pl.when(r == 1)
    def _():
        for load in att_loads:
            load.wait()
        each(half_rows, attend_row)

    def to_pair(which, src):
        return remote(
            slabs.at[which, src * 2 + core],
            slabs.at[which, src * 2 + core],
            c_send.at[which, src],
            c_recv.at[which, src],
            r, i, t + 1 - 2 * core,
        )

    def from_pair(which, src):
        drain(slabs.at[which, src * 2 + 1 - core], c_recv.at[which, src])

    def over(which, step):
        dst = (px + step) % pairs
        return remote(
            slabs.at[which, t],
            slabs.at[which, t],
            x_send.at[which, step],
            x_recv.at[which, px],
            r, i, dst * 2 + core,
        )

    @pl.when(active)
    def _():
        own = pltpu.make_async_copy(piece(r, i), slabs.at[r, t, i], loc.at[1])
        own.start()
        for which in range(2):
            @pl.when(r != which)
            def _(which=which):
                drain(slabs.at[which, t], hid_recv.at[which])

            @pl.when(r == which)
            def _(which=which):
                drain(slabs.at[which, t, pl.ds(0, n - 1)], hid_recv.at[which])
                own.wait()

            for step in range(1, pairs):
                over(which, step).start()
            to_pair(which, px).start()

    drain(ogs.at[pl.ds(0, n - 1)], og_recv)
    og_local.wait()
    for load in loads:
        load.wait()

    chunk = min(512, full)
    part_rows = og.shape[0] // 2
    block_rows = q * part_rows
    own_half = pl.ds(pl.multiple_of(r * part_rows, part_rows), part_rows)

    def fill_part(g):
        tokens = ogs[pl.ds(g * q, q), own_half, :].reshape(block_rows, heads)

        def columns(k):
            at = pl.ds(pl.multiple_of(k * chunk, chunk), chunk)
            parts[g, :, at] = lax.dot_general(
                tokens,
                master_v[at, :].astype(jnp.bfloat16),
                (((1,), (1,)), ((), ())),
                preferred_element_type=jnp.float32,
            ).astype(jnp.bfloat16)

        each(full // chunk, columns)

    mine = pltpu.make_async_copy(parts.at[t], slots.at[t], loc.at[0])

    def send_part(k):
        g = (t + 1 + k) % m
        fill_part(g)
        remote(parts.at[g], slots.at[t], p_send, p_recv, r, i, g).start()

    each(m - 1, send_part)
    fill_part(t)
    mine.start()

    @pl.when(r == 1)
    def _():
        each(replica_rows - half_rows, lambda k: attend_row(half_rows + k))

    def send_sum(j):
        slot = r * n + i if split else i
        remote(sums.at[j], val_slots.at[slot], v_send, v_recv, 1, j, t).start()

    @pl.when(active)
    def _():
        for which in range(2):
            for step in range(1, pairs):
                src = (px + step) % pairs
                drain(slabs.at[which, src * 2 + core], x_recv.at[which, src])
                to_pair(which, src).start()
        for src in range(pairs):
            from_pair(0, src)

        tile = min(256, width)

        def update(k):
            at = pl.ds(pl.multiple_of(k * tile, tile), tile)
            gradient = jnp.zeros((tile, heads), jnp.float32)
            for g in range(m):
                gradient = gradient + lax.dot_general(
                    slabs[0, g, :, :, at].reshape(n * rows, tile),
                    ogs[:, g * rows : (g + 1) * rows, :].reshape(n * rows, heads),
                    (((0,), (0,)), ((), ())),
                    preferred_element_type=jnp.float32,
                )
            held = pl.ds(pl.multiple_of(first + k * tile, tile), tile)
            fresh[at, :] = adam_fresh(master_v[held, :], moment1_v[at, :], moment2_v[at, :], gradient)

        each(width // tile, update)

    drain(slots.at[pl.ds(0, m - 1)], p_recv)
    mine.wait()
    total_of(slots, m, reduced, 16)

    def place(j):
        return back.at[own_half, pl.ds(pl.multiple_of((j % q) * full, full), full)]

    def block(k):
        return reduced.at[pl.ds(pl.multiple_of(k * part_rows, part_rows), part_rows)]

    def send_block(k):
        @pl.when((r == 1) | (t * q + k != i))
        def _():
            remote(block(k), place(i), b_send, b_recv, 0, t * q + k, home).start()

    each(q, send_block)

    @pl.when(active)
    def _():
        for src in range(pairs):
            from_pair(1, src)
        for g in range(m):
            sums[:, g * rows : (g + 1) * rows, :] = (
                jnp.dot(
                    slabs[1, g].reshape(n * rows, width), fresh[...], preferred_element_type=jnp.float32
                )
                .astype(jnp.bfloat16)
                .reshape(n, rows, heads)
            )
        each(n - 1, lambda k: send_sum((i + 1 + k) % n))

        @pl.when(r == 0)
        def _():
            send_sum(i)

    @pl.when((r == 0) & (home == t))
    def _():
        keep = pltpu.make_async_copy(block(i % q), place(i), loc.at[0])
        keep.start()
        keep.wait()
        drain(reduced, b_recv)
        if q > 1:
            drain(reduced.at[pl.ds(0, (q - 1) * part_rows)], b_recv)
            drain(reduced.at[pl.ds(0, (q - 1) * part_rows)], b_send)

    @pl.when((r == 0) & (home != t))
    def _():
        drain(back, b_recv)
        drain(reduced, b_send)

    @pl.when(r == 0)
    def _():
        if split:
            drain(val_slots.at[pl.ds(0, n)], v_send)

    @pl.when(r == 1)
    def _():
        kept = pltpu.make_async_copy(sums.at[i], val_slots.at[n + i if split else i], loc.at[0])
        kept.start()
        drain(val_slots.at[pl.ds(0, sources - 1)], v_recv)
        kept.wait()
        total_of(val_slots, sources, vals, 16)
        each(replica_rows, finish_row)
        drain(val_slots.at[pl.ds(0, n - 1)], v_send)
        drain(reduced, b_send)

    drain(slots.at[pl.ds(0, m - 1)], p_send)

    @pl.when(active)
    def _():
        for which in range(2):
            for step in range(1, pairs):
                over(which, step).wait_send()
            for src in range(pairs):
                to_pair(which, src).wait_send()

    for role in targets:
        @pl.when(r != role)
        def _(role=role):
            drain(slabs.at[role, t], hid_send.at[role])

        @pl.when(r == role)
        def _(role=role):
            drain(slabs.at[role, t, pl.ds(0, n - 1)], hid_send.at[role])

    drain(ogs.at[pl.ds(0, n - 1)], og_send)


def fused(hid, og, master, moment1, moment2, queries, keys, k_cache, v_cache, lens, n, m):
    q = n // m
    full, heads = master.shape
    tokens = og.shape[0]
    split = full % 256 == 0
    width = full // 2 if split else full
    dma = pltpu.SemaphoreType.DMA
    anywhere = pl.BlockSpec(memory_space=pltpu.HBM)
    half = pltpu.VMEM((width, heads), jnp.float32)
    block = pltpu.VMEM((m, q * (tokens // 2), full), jnp.bfloat16)
    return pl.pallas_call(
        functools.partial(fused_kernel, n, m, split),
        out_shape=(
            jax.ShapeDtypeStruct((tokens, q * full), jnp.bfloat16),
            jax.ShapeDtypeStruct(queries.shape, jnp.bfloat16),
        ),
        in_specs=[anywhere] * 9 + [pl.BlockSpec(memory_space=pltpu.SMEM)],
        out_specs=(anywhere, pl.BlockSpec(memory_space=pltpu.VMEM)),
        scratch_shapes=[
            pltpu.VMEM((2, m, n, tokens // m, width), jnp.bfloat16),
            pltpu.VMEM((n, tokens, heads), jnp.bfloat16),
            pltpu.VMEM((full, heads), jnp.float32),
            half,
            half,
            pltpu.VMEM((width, heads), jnp.bfloat16),
            pltpu.VMEM((n, tokens, heads), jnp.bfloat16),
            block,
            block,
            pltpu.VMEM((q * (tokens // 2), full), jnp.bfloat16),
            pltpu.VMEM((n * (2 if split else 1), tokens, heads), jnp.bfloat16),
            dma, dma, dma((2,)), dma((2,)), dma((5,)),
            dma((2, m // 2)), dma((2, m // 2)), dma((2, m // 2)), dma((2, m // 2)),
            dma, dma, dma, dma, dma, dma,
            pltpu.VMEM((tokens, heads), jnp.bfloat16),
            pltpu.VMEM(queries.shape, queries.dtype),
            pltpu.VMEM(keys.shape, keys.dtype),
            pltpu.VMEM(k_cache.shape, k_cache.dtype),
            pltpu.VMEM(v_cache.shape, v_cache.dtype),
            pltpu.VMEM(queries.shape, jnp.float32),
            pltpu.VMEM(queries.shape[:3] + (tokens,), jnp.bfloat16),
            dma((4,)),
        ],
        compiler_params=pltpu.CompilerParams(
            collective_id=0, has_side_effects=True, vmem_limit_bytes=60 * 2**20
        ),
    )(hid, og, master, moment1, moment2, queries, keys, k_cache, v_cache, lens)


def local(
    hidden, out_grad, master, moment1, moment2, queries, new_keys, k_cache, v_cache, cache_len
):
    is_learner = lax.axis_index("role") == 0
    n, m = lax.axis_size("dp"), lax.axis_size("tp")
    replica_rows = cache_len.shape[0]
    heads_here = out_grad.shape[1] // HD
    share = QH // KVH
    asked = queries.reshape(STEPS, replica_rows, heads_here, share, HD).transpose(1, 2, 0, 3, 4)
    learner_rows, attended = fused(
        hidden[0],
        out_grad,
        master,
        moment1,
        moment2,
        asked.reshape(replica_rows, heads_here, STEPS * share, HD),
        new_keys.reshape(STEPS * replica_rows, heads_here * HD),
        k_cache,
        v_cache,
        cache_len,
        n,
        m,
    )
    decoded = attended.reshape(replica_rows, heads_here, STEPS, share, HD).transpose(2, 0, 1, 3, 4)
    result = jnp.where(is_learner, learner_rows, decoded.reshape(learner_rows.shape))
    return result[None]


def solution(mesh):
    return jax.shard_map(
        local,
        mesh=mesh,
        in_specs=(
            P("role", "dp", None),
            P("dp", "tp"),
            P("dp", "tp"),
            P("dp", "tp"),
            P("dp", "tp"),
            P(None, "dp", "tp"),
            P(None, "dp", "tp"),
            P("dp", None, "tp"),
            P("dp", None, "tp"),
            P("dp"),
        ),
        out_specs=P("role", "dp", "tp"),
        check_vma=False,
    )
```

```python
import functools

import jax
import jax.numpy as jnp
from jax import lax
from jax.experimental import pallas as pl
from jax.experimental.pallas import tpu as pltpu
from jax.sharding import PartitionSpec as P

D = 8192
KVH = 8
QH = 64
HD = 128
STEPS = 8


beta_one = 0.9
beta_two = 0.95
adam_eps = 1e-08
bias_one = 1.0 - 0.9**10
bias_two = 1.0 - 0.95**10
neg_fill = -1e30


def adam_fresh(master, moment1, moment2, gradient):
    step_size = 2.0 * D ** (-0.5)
    first = beta_one * moment1 + (1.0 - beta_one) * gradient
    second = beta_two * moment2 + (1.0 - beta_two) * gradient * gradient
    change = first / bias_one / (jnp.sqrt(second / bias_two) + adam_eps)
    return (master - step_size * change).astype(jnp.bfloat16)


MESH = pl.DeviceIdType.MESH


def position():
    return lax.axis_index("role"), lax.axis_index("dp"), lax.axis_index("tp")


def signal(semaphore, role, row, col):
    pl.semaphore_signal(semaphore, inc=1, device_id=(role, row, col), device_id_type=MESH)


def remote(src, dst, send, recv, role, row, col):
    return pltpu.make_async_remote_copy(
        src_ref=src,
        dst_ref=dst,
        send_sem=send,
        recv_sem=recv,
        device_id=(role, row, col),
        device_id_type=MESH,
    )


def drain(ref, semaphore):
    pltpu.make_async_copy(ref, ref, semaphore).wait()


def each(count, body):
    def step(k, carry):
        body(k)
        return carry

    lax.fori_loop(0, count, step, 0)


def total_of(slots, count, out, tile):
    def chunk(k):
        at = pl.ds(pl.multiple_of(k * tile, tile), tile)
        total = slots[0, at, :].astype(jnp.float32)
        for s in range(1, count):
            total = total + slots[s, at, :].astype(jnp.float32)
        out[at, :] = total.astype(out.dtype)

    each(out.shape[0] // tile, chunk)


def fused_kernel(
    n, m, split, hid, og, master, moment1, moment2, queries, keys, k_cache, v_cache, lens, back, att,
    slabs, ogs, master_v, moment1_v, moment2_v, fresh, sums, parts, slots, reduced, val_slots,
    og_send, og_recv, hid_send, hid_recv, loc, x_send, x_recv, c_send, c_recv,
    p_send, p_recv, b_send, b_recv, v_send, v_recv,
    vals, queries_v, keys_v, k_v, v_v, cache_out, fresh_wts, att_sem,
):
    r, i, t = position()
    q = n // m
    rows, width = slabs.shape[3], slabs.shape[4]
    full = master.shape[0]
    heads = og.shape[1]
    home = i // q
    pairs = m // 2
    px, core = t // 2, t % 2
    sources = val_slots.shape[0]
    active = (r == 1) | split

    loads = [pltpu.make_async_copy(master, master_v, loc.at[2])]
    first = pl.multiple_of((r * width) if split else 0, width)
    for k, (src, dst) in enumerate(((moment1, moment1_v), (moment2, moment2_v))):
        loads.append(pltpu.make_async_copy(src.at[pl.ds(first, width)], dst, loc.at[3 + k]))
    for load in loads:
        load.start()

    att_loads = [
        pltpu.make_async_copy(src, dst, att_sem.at[k])
        for k, (src, dst) in enumerate(
            ((queries, queries_v), (keys, keys_v), (k_cache, k_v), (v_cache, v_v))
        )
    ]

    @pl.when(r == 1)
    def _():
        for load in att_loads:
            load.start()

    barrier = pltpu.get_barrier_semaphore()

    def greet(k):
        @pl.when(k != r * n + i)
        def _():
            signal(barrier, k // n, k % n, t)

    def greet_tp(k):
        signal(barrier, r, i, (t + 1 + k) % m)

    def greet_far(k):
        @pl.when(t * q + k != i)
        def _():
            signal(barrier, 0, t * q + k, home)

        signal(barrier, 1, t * q + k, home)

    each(2 * n, greet)
    each(m - 1, greet_tp)

    @pl.when(r == 0)
    def _():
        each(q, greet_far)
        pl.semaphore_wait(barrier, 2 * n - 1 + m - 1 + q - jnp.where(home == t, 1, 0))

    @pl.when(r == 1)
    def _():
        pl.semaphore_wait(barrier, 2 * n - 1 + m - 1 + q)

    def piece(role, j):
        start = j * full + (role * width if split else 0)
        return hid.at[pl.ds(pl.multiple_of(t * rows, rows), rows), pl.ds(pl.multiple_of(start, width), width)]

    def send_og(k):
        j = (i + k) % n
        remote(og, ogs.at[i], og_send, og_recv, r, j, t).start()

    def send_hid(role, j):
        remote(piece(role, j), slabs.at[r, t, i], hid_send.at[role], hid_recv.at[r], role, j, t).start()

    each(n - 1, lambda k: send_og(k + 1))
    targets = (0, 1) if split else (1,)
    for role in targets:
        each(n - 1, lambda k, role=role: send_hid(role, (i + k + 1) % n))

        @pl.when(r != role)
        def _(role=role):
            send_hid(role, i)

    og_local = pltpu.make_async_copy(og, ogs.at[i], loc.at[0])
    og_local.start()

    replica_rows, kv_heads, asked = queries.shape[:3]
    half_rows = replica_rows // 2

    def attend_row(row):
        for k in range(kv_heads):
            at = slice(k * HD, (k + 1) * HD)
            cache_score, fresh_score = [
                lax.dot_general(
                    queries_v[row, k], known, (((1,), (1,)), ((), ())), preferred_element_type=jnp.float32
                )
                * HD ** (-0.5)
                for known in (k_v[row, :, at], keys_v[:, at])
            ]
            place = lax.broadcasted_iota(jnp.int32, cache_score.shape, 1)
            cache_score = jnp.where(place < lens[row], cache_score, neg_fill)
            token = lax.broadcasted_iota(jnp.int32, fresh_score.shape, 1)
            step = lax.broadcasted_iota(jnp.int32, fresh_score.shape, 0) // (asked // STEPS)
            seen = (token % replica_rows == row) & (token // replica_rows <= step)
            fresh_score = jnp.where(seen, fresh_score, neg_fill)
            top = jnp.maximum(
                jnp.max(cache_score, axis=-1, keepdims=True), jnp.max(fresh_score, axis=-1, keepdims=True)
            )
            cache_exp = jnp.exp(cache_score - top)
            fresh_exp = jnp.exp(fresh_score - top)
            total = jnp.sum(cache_exp, axis=-1, keepdims=True) + jnp.sum(fresh_exp, axis=-1, keepdims=True)
            cache_wts = (cache_exp / total).astype(jnp.bfloat16)
            fresh_wts[row, k] = (fresh_exp / total).astype(jnp.bfloat16)
            cache_out[row, k] = jnp.dot(cache_wts, v_v[row, :, at], preferred_element_type=jnp.float32)

    def finish_row(row):
        for k in range(kv_heads):
            new = jnp.dot(
                fresh_wts[row, k], vals[:, k * HD : (k + 1) * HD], preferred_element_type=jnp.float32
            )
            att[row, k] = (cache_out[row, k] + new).astype(att.dtype)

    drain(ogs.at[pl.ds(0, n - 1)], og_recv)
    og_local.wait()
    for load in loads:
        load.wait()

    chunk = min(512, full)
    part_rows = og.shape[0] // 2
    block_rows = q * part_rows
    own_half = pl.ds(pl.multiple_of(r * part_rows, part_rows), part_rows)

    def fill_part(g):
        tokens = ogs[pl.ds(g * q, q), own_half, :].reshape(block_rows, heads)

        def columns(k):
            at = pl.ds(pl.multiple_of(k * chunk, chunk), chunk)
            parts[g, :, at] = lax.dot_general(
                tokens,
                master_v[at, :].astype(jnp.bfloat16),
                (((1,), (1,)), ((), ())),
                preferred_element_type=jnp.float32,
            ).astype(jnp.bfloat16)

        each(full // chunk, columns)

    mine = pltpu.make_async_copy(parts.at[t], slots.at[t], loc.at[0])

    def send_part(k):
        g = (t + 1 + k) % m
        fill_part(g)
        remote(parts.at[g], slots.at[t], p_send, p_recv, r, i, g).start()

    each(m - 1, send_part)
    fill_part(t)
    mine.start()

    @pl.when(r == 1)
    def _():
        for load in att_loads:
            load.wait()
        each(half_rows, attend_row)

    def to_pair(which, src):
        return remote(
            slabs.at[which, src * 2 + core],
            slabs.at[which, src * 2 + core],
            c_send.at[which, src],
            c_recv.at[which, src],
            r, i, t + 1 - 2 * core,
        )

    def from_pair(which, src):
        drain(slabs.at[which, src * 2 + 1 - core], c_recv.at[which, src])

    def over(which, step):
        dst = (px + step) % pairs
        return remote(
            slabs.at[which, t],
            slabs.at[which, t],
            x_send.at[which, step],
            x_recv.at[which, px],
            r, i, dst * 2 + core,
        )

    @pl.when(active)
    def _():
        own = pltpu.make_async_copy(piece(r, i), slabs.at[r, t, i], loc.at[1])
        own.start()
        for which in range(2):
            @pl.when(r != which)
            def _(which=which):
                drain(slabs.at[which, t], hid_recv.at[which])

            @pl.when(r == which)
            def _(which=which):
                drain(slabs.at[which, t, pl.ds(0, n - 1)], hid_recv.at[which])
                own.wait()

            for step in range(1, pairs):
                over(which, step).start()
            to_pair(which, px).start()

    @pl.when(r == 1)
    def _():
        each(replica_rows - half_rows, lambda k: attend_row(half_rows + k))

    def send_sum(j):
        slot = r * n + i if split else i
        remote(sums.at[j], val_slots.at[slot], v_send, v_recv, 1, j, t).start()

    @pl.when(active)
    def _():
        for which in range(2):
            for step in range(1, pairs):
                src = (px + step) % pairs
                drain(slabs.at[which, src * 2 + core], x_recv.at[which, src])
                to_pair(which, src).start()
        for src in range(pairs):
            from_pair(0, src)

        tile = min(256, width)

        def update(k):
            at = pl.ds(pl.multiple_of(k * tile, tile), tile)
            gradient = jnp.zeros((tile, heads), jnp.float32)
            for g in range(m):
                gradient = gradient + lax.dot_general(
                    slabs[0, g, :, :, at].reshape(n * rows, tile),
                    ogs[:, g * rows : (g + 1) * rows, :].reshape(n * rows, heads),
                    (((0,), (0,)), ((), ())),
                    preferred_element_type=jnp.float32,
                )
            held = pl.ds(pl.multiple_of(first + k * tile, tile), tile)
            fresh[at, :] = adam_fresh(master_v[held, :], moment1_v[at, :], moment2_v[at, :], gradient)

        each(width // tile, update)
        for src in range(pairs):
            from_pair(1, src)
        for g in range(m):
            sums[:, g * rows : (g + 1) * rows, :] = (
                jnp.dot(
                    slabs[1, g].reshape(n * rows, width), fresh[...], preferred_element_type=jnp.float32
                )
                .astype(jnp.bfloat16)
                .reshape(n, rows, heads)
            )
        each(n - 1, lambda k: send_sum((i + 1 + k) % n))

        @pl.when(r == 0)
        def _():
            send_sum(i)

    drain(slots.at[pl.ds(0, m - 1)], p_recv)
    mine.wait()
    total_of(slots, m, reduced, 16)

    def place(j):
        return back.at[own_half, pl.ds(pl.multiple_of((j % q) * full, full), full)]

    def block(k):
        return reduced.at[pl.ds(pl.multiple_of(k * part_rows, part_rows), part_rows)]

    def send_block(k):
        @pl.when((r == 1) | (t * q + k != i))
        def _():
            remote(block(k), place(i), b_send, b_recv, 0, t * q + k, home).start()

    each(q, send_block)

    @pl.when((r == 0) & (home == t))
    def _():
        keep = pltpu.make_async_copy(block(i % q), place(i), loc.at[0])
        keep.start()
        keep.wait()
        drain(reduced, b_recv)
        if q > 1:
            drain(reduced.at[pl.ds(0, (q - 1) * part_rows)], b_recv)
            drain(reduced.at[pl.ds(0, (q - 1) * part_rows)], b_send)

    @pl.when((r == 0) & (home != t))
    def _():
        drain(back, b_recv)
        drain(reduced, b_send)

    @pl.when(r == 0)
    def _():
        if split:
            drain(val_slots.at[pl.ds(0, n)], v_send)

    @pl.when(r == 1)
    def _():
        kept = pltpu.make_async_copy(sums.at[i], val_slots.at[n + i if split else i], loc.at[0])
        kept.start()
        drain(val_slots.at[pl.ds(0, sources - 1)], v_recv)
        kept.wait()
        total_of(val_slots, sources, vals, 16)
        each(replica_rows, finish_row)
        drain(val_slots.at[pl.ds(0, n - 1)], v_send)
        drain(reduced, b_send)

    drain(slots.at[pl.ds(0, m - 1)], p_send)

    @pl.when(active)
    def _():
        for which in range(2):
            for step in range(1, pairs):
                over(which, step).wait_send()
            for src in range(pairs):
                to_pair(which, src).wait_send()

    for role in targets:
        @pl.when(r != role)
        def _(role=role):
            drain(slabs.at[role, t], hid_send.at[role])

        @pl.when(r == role)
        def _(role=role):
            drain(slabs.at[role, t, pl.ds(0, n - 1)], hid_send.at[role])

    drain(ogs.at[pl.ds(0, n - 1)], og_send)


def fused(hid, og, master, moment1, moment2, queries, keys, k_cache, v_cache, lens, n, m):
    q = n // m
    full, heads = master.shape
    tokens = og.shape[0]
    split = full % 256 == 0
    width = full // 2 if split else full
    dma = pltpu.SemaphoreType.DMA
    anywhere = pl.BlockSpec(memory_space=pltpu.HBM)
    half = pltpu.VMEM((width, heads), jnp.float32)
    block = pltpu.VMEM((m, q * (tokens // 2), full), jnp.bfloat16)
    return pl.pallas_call(
        functools.partial(fused_kernel, n, m, split),
        out_shape=(
            jax.ShapeDtypeStruct((tokens, q * full), jnp.bfloat16),
            jax.ShapeDtypeStruct(queries.shape, jnp.bfloat16),
        ),
        in_specs=[anywhere] * 9 + [pl.BlockSpec(memory_space=pltpu.SMEM)],
        out_specs=(anywhere, pl.BlockSpec(memory_space=pltpu.VMEM)),
        scratch_shapes=[
            pltpu.VMEM((2, m, n, tokens // m, width), jnp.bfloat16),
            pltpu.VMEM((n, tokens, heads), jnp.bfloat16),
            pltpu.VMEM((full, heads), jnp.float32),
            half,
            half,
            pltpu.VMEM((width, heads), jnp.bfloat16),
            pltpu.VMEM((n, tokens, heads), jnp.bfloat16),
            block,
            block,
            pltpu.VMEM((q * (tokens // 2), full), jnp.bfloat16),
            pltpu.VMEM((n * (2 if split else 1), tokens, heads), jnp.bfloat16),
            dma, dma, dma((2,)), dma((2,)), dma((5,)),
            dma((2, m // 2)), dma((2, m // 2)), dma((2, m // 2)), dma((2, m // 2)),
            dma, dma, dma, dma, dma, dma,
            pltpu.VMEM((tokens, heads), jnp.bfloat16),
            pltpu.VMEM(queries.shape, queries.dtype),
            pltpu.VMEM(keys.shape, keys.dtype),
            pltpu.VMEM(k_cache.shape, k_cache.dtype),
            pltpu.VMEM(v_cache.shape, v_cache.dtype),
            pltpu.VMEM(queries.shape, jnp.float32),
            pltpu.VMEM(queries.shape[:3] + (tokens,), jnp.bfloat16),
            dma((4,)),
        ],
        compiler_params=pltpu.CompilerParams(
            collective_id=0, has_side_effects=True, vmem_limit_bytes=60 * 2**20
        ),
    )(hid, og, master, moment1, moment2, queries, keys, k_cache, v_cache, lens)


def local(
    hidden, out_grad, master, moment1, moment2, queries, new_keys, k_cache, v_cache, cache_len
):
    is_learner = lax.axis_index("role") == 0
    n, m = lax.axis_size("dp"), lax.axis_size("tp")
    replica_rows = cache_len.shape[0]
    heads_here = out_grad.shape[1] // HD
    share = QH // KVH
    asked = queries.reshape(STEPS, replica_rows, heads_here, share, HD).transpose(1, 2, 0, 3, 4)
    learner_rows, attended = fused(
        hidden[0],
        out_grad,
        master,
        moment1,
        moment2,
        asked.reshape(replica_rows, heads_here, STEPS * share, HD),
        new_keys.reshape(STEPS * replica_rows, heads_here * HD),
        k_cache,
        v_cache,
        cache_len,
        n,
        m,
    )
    decoded = attended.reshape(replica_rows, heads_here, STEPS, share, HD).transpose(2, 0, 1, 3, 4)
    result = jnp.where(is_learner, learner_rows, decoded.reshape(learner_rows.shape))
    return result[None]


def solution(mesh):
    return jax.shard_map(
        local,
        mesh=mesh,
        in_specs=(
            P("role", "dp", None),
            P("dp", "tp"),
            P("dp", "tp"),
            P("dp", "tp"),
            P("dp", "tp"),
            P(None, "dp", "tp"),
            P(None, "dp", "tp"),
            P("dp", None, "tp"),
            P("dp", None, "tp"),
            P("dp"),
        ),
        out_specs=P("role", "dp", "tp"),
        check_vma=False,
    )
```

```python
import functools

import jax
import jax.numpy as jnp
from jax import lax
from jax.experimental import pallas as pl
from jax.experimental.pallas import tpu as pltpu
from jax.sharding import PartitionSpec as P

D = 8192
KVH = 8
QH = 64
HD = 128
STEPS = 8


beta_one = 0.9
beta_two = 0.95
adam_eps = 1e-08
bias_one = 1.0 - 0.9**10
bias_two = 1.0 - 0.95**10
neg_fill = -1e30


def adam_fresh(master, moment1, moment2, gradient):
    step_size = 2.0 * D ** (-0.5)
    first = beta_one * moment1 + (1.0 - beta_one) * gradient
    second = beta_two * moment2 + (1.0 - beta_two) * gradient * gradient
    change = first / bias_one / (jnp.sqrt(second / bias_two) + adam_eps)
    return (master - step_size * change).astype(jnp.bfloat16)


MESH = pl.DeviceIdType.MESH


def position():
    return lax.axis_index("role"), lax.axis_index("dp"), lax.axis_index("tp")


def signal(semaphore, role, row, col):
    pl.semaphore_signal(semaphore, inc=1, device_id=(role, row, col), device_id_type=MESH)


def remote(src, dst, send, recv, role, row, col):
    return pltpu.make_async_remote_copy(
        src_ref=src,
        dst_ref=dst,
        send_sem=send,
        recv_sem=recv,
        device_id=(role, row, col),
        device_id_type=MESH,
    )


def drain(ref, semaphore):
    pltpu.make_async_copy(ref, ref, semaphore).wait()


def each(count, body):
    def step(k, carry):
        body(k)
        return carry

    lax.fori_loop(0, count, step, 0)


def total_of(slots, count, out, tile):
    def chunk(k):
        at = pl.ds(pl.multiple_of(k * tile, tile), tile)
        total = slots[0, at, :].astype(jnp.float32)
        for s in range(1, count):
            total = total + slots[s, at, :].astype(jnp.float32)
        out[at, :] = total.astype(out.dtype)

    each(out.shape[0] // tile, chunk)


def fused_kernel(
    n, m, split, hid, og, master, moment1, moment2, queries, keys, k_cache, v_cache, lens, back, att,
    slabs, ogs, master_v, moment1_v, moment2_v, fresh, sums, parts, slots, reduced, val_slots,
    og_send, og_recv, hid_send, hid_recv, loc, x_send, x_recv, c_send, c_recv,
    p_send, p_recv, b_send, b_recv, v_send, v_recv,
    vals, queries_v, asked_v, keys_v, k_v, v_v, cache_out, fresh_wts, att_sem,
):
    r, i, t = position()
    q = n // m
    rows, width = slabs.shape[3], slabs.shape[4]
    full = master.shape[0]
    heads = og.shape[1]
    home = i // q
    pairs = m // 2
    px, core = t // 2, t % 2
    sources = val_slots.shape[0]
    active = (r == 1) | split

    loads = [pltpu.make_async_copy(master, master_v, loc.at[2])]
    first = pl.multiple_of((r * width) if split else 0, width)
    for k, (src, dst) in enumerate(((moment1, moment1_v), (moment2, moment2_v))):
        loads.append(pltpu.make_async_copy(src.at[pl.ds(first, width)], dst, loc.at[3 + k]))
    for load in loads:
        load.start()

    att_loads = [
        pltpu.make_async_copy(src, dst, att_sem.at[k])
        for k, (src, dst) in enumerate(
            ((queries, queries_v), (keys, keys_v), (k_cache, k_v), (v_cache, v_v))
        )
    ]

    @pl.when(r == 1)
    def _():
        for load in att_loads:
            load.start()

    barrier = pltpu.get_barrier_semaphore()

    def greet(k):
        @pl.when(k != r * n + i)
        def _():
            signal(barrier, k // n, k % n, t)

    def greet_tp(k):
        signal(barrier, r, i, (t + 1 + k) % m)

    def greet_far(k):
        @pl.when(t * q + k != i)
        def _():
            signal(barrier, 0, t * q + k, home)

        signal(barrier, 1, t * q + k, home)

    each(2 * n, greet)
    each(m - 1, greet_tp)

    @pl.when(r == 0)
    def _():
        each(q, greet_far)
        pl.semaphore_wait(barrier, 2 * n - 1 + m - 1 + q - jnp.where(home == t, 1, 0))

    @pl.when(r == 1)
    def _():
        pl.semaphore_wait(barrier, 2 * n - 1 + m - 1 + q)

    def piece(role, j):
        start = j * full + (role * width if split else 0)
        return hid.at[pl.ds(pl.multiple_of(t * rows, rows), rows), pl.ds(pl.multiple_of(start, width), width)]

    def send_og(k):
        j = (i + k) % n
        remote(og, ogs.at[i], og_send, og_recv, r, j, t).start()

    def send_hid(role, j):
        remote(piece(role, j), slabs.at[r, t, i], hid_send.at[role], hid_recv.at[r], role, j, t).start()

    each(n - 1, lambda k: send_og(k + 1))
    targets = (0, 1) if split else (1,)
    for role in targets:
        each(n - 1, lambda k, role=role: send_hid(role, (i + k + 1) % n))

        @pl.when(r != role)
        def _(role=role):
            send_hid(role, i)

    og_local = pltpu.make_async_copy(og, ogs.at[i], loc.at[0])
    og_local.start()

    replica_rows, kv_heads, asked = asked_v.shape[:3]
    share = asked // STEPS
    half_rows = replica_rows // 2

    def attend_row(row):
        for k in range(kv_heads):
            at = slice(k * HD, (k + 1) * HD)
            cache_score, fresh_score = [
                lax.dot_general(
                    asked_v[row, k].astype(jnp.bfloat16), known, (((1,), (1,)), ((), ())), preferred_element_type=jnp.float32
                )
                * HD ** (-0.5)
                for known in (k_v[row, :, at], keys_v[:, at])
            ]
            place = lax.broadcasted_iota(jnp.int32, cache_score.shape, 1)
            cache_score = jnp.where(place < lens[row], cache_score, neg_fill)
            token = lax.broadcasted_iota(jnp.int32, fresh_score.shape, 1)
            step = lax.broadcasted_iota(jnp.int32, fresh_score.shape, 0) // share
            seen = (token % replica_rows == row) & (token // replica_rows <= step)
            fresh_score = jnp.where(seen, fresh_score, neg_fill)
            top = jnp.maximum(
                jnp.max(cache_score, axis=-1, keepdims=True), jnp.max(fresh_score, axis=-1, keepdims=True)
            )
            cache_exp = jnp.exp(cache_score - top)
            fresh_exp = jnp.exp(fresh_score - top)
            total = jnp.sum(cache_exp, axis=-1, keepdims=True) + jnp.sum(fresh_exp, axis=-1, keepdims=True)
            cache_wts = (cache_exp / total).astype(jnp.bfloat16)
            fresh_wts[row, k] = (fresh_exp / total).astype(jnp.bfloat16)
            cache_out[row, k] = jnp.dot(cache_wts, v_v[row, :, at], preferred_element_type=jnp.float32)

    def finish_row(row):
        for k in range(kv_heads):
            new = jnp.dot(
                fresh_wts[row, k], vals[:, k * HD : (k + 1) * HD], preferred_element_type=jnp.float32
            )
            att[row, k] = (cache_out[row, k] + new).astype(att.dtype)

    drain(ogs.at[pl.ds(0, n - 1)], og_recv)
    og_local.wait()
    for load in loads:
        load.wait()

    chunk = min(512, full)
    part_rows = og.shape[0] // 2
    block_rows = q * part_rows
    own_half = pl.ds(pl.multiple_of(r * part_rows, part_rows), part_rows)

    def fill_part(g):
        tokens = ogs[pl.ds(g * q, q), own_half, :].reshape(block_rows, heads)

        def columns(k):
            at = pl.ds(pl.multiple_of(k * chunk, chunk), chunk)
            parts[g, :, at] = lax.dot_general(
                tokens,
                master_v[at, :].astype(jnp.bfloat16),
                (((1,), (1,)), ((), ())),
                preferred_element_type=jnp.float32,
            ).astype(jnp.bfloat16)

        each(full // chunk, columns)

    mine = pltpu.make_async_copy(parts.at[t], slots.at[t], loc.at[0])

    def send_part(k):
        g = (t + 1 + k) % m
        fill_part(g)
        remote(parts.at[g], slots.at[t], p_send, p_recv, r, i, g).start()

    each(m - 1, send_part)
    fill_part(t)
    mine.start()

    @pl.when(r == 1)
    def _():
        for load in att_loads:
            load.wait()

        for s in range(STEPS):
            for k in range(kv_heads):
                for h in range(share):
                    at = (k * share + h) * HD
                    asked_v[:, k, s * share + h, :] = queries_v[s, :, at : at + HD].astype(jnp.float32)

        each(half_rows, attend_row)

    def to_pair(which, src):
        return remote(
            slabs.at[which, src * 2 + core],
            slabs.at[which, src * 2 + core],
            c_send.at[which, src],
            c_recv.at[which, src],
            r, i, t + 1 - 2 * core,
        )

    def from_pair(which, src):
        drain(slabs.at[which, src * 2 + 1 - core], c_recv.at[which, src])

    def over(which, step):
        dst = (px + step) % pairs
        return remote(
            slabs.at[which, t],
            slabs.at[which, t],
            x_send.at[which, step],
            x_recv.at[which, px],
            r, i, dst * 2 + core,
        )

    @pl.when(active)
    def _():
        own = pltpu.make_async_copy(piece(r, i), slabs.at[r, t, i], loc.at[1])
        own.start()
        for which in range(2):
            @pl.when(r != which)
            def _(which=which):
                drain(slabs.at[which, t], hid_recv.at[which])

            @pl.when(r == which)
            def _(which=which):
                drain(slabs.at[which, t, pl.ds(0, n - 1)], hid_recv.at[which])
                own.wait()

            for step in range(1, pairs):
                over(which, step).start()
            to_pair(which, px).start()

    @pl.when(r == 1)
    def _():
        each(replica_rows - half_rows, lambda k: attend_row(half_rows + k))

    def send_sum(j):
        slot = r * n + i if split else i
        remote(sums.at[j], val_slots.at[slot], v_send, v_recv, 1, j, t).start()

    @pl.when(active)
    def _():
        for which in range(2):
            for step in range(1, pairs):
                src = (px + step) % pairs
                drain(slabs.at[which, src * 2 + core], x_recv.at[which, src])
                to_pair(which, src).start()
        for src in range(pairs):
            from_pair(0, src)

        tile = min(256, width)

        def update(k):
            at = pl.ds(pl.multiple_of(k * tile, tile), tile)
            gradient = jnp.zeros((tile, heads), jnp.float32)
            for g in range(m):
                gradient = gradient + lax.dot_general(
                    slabs[0, g, :, :, at].reshape(n * rows, tile),
                    ogs[:, g * rows : (g + 1) * rows, :].reshape(n * rows, heads),
                    (((0,), (0,)), ((), ())),
                    preferred_element_type=jnp.float32,
                )
            held = pl.ds(pl.multiple_of(first + k * tile, tile), tile)
            fresh[at, :] = adam_fresh(master_v[held, :], moment1_v[at, :], moment2_v[at, :], gradient)

        each(width // tile, update)
        for src in range(pairs):
            from_pair(1, src)
        for g in range(m):
            sums[:, g * rows : (g + 1) * rows, :] = (
                jnp.dot(
                    slabs[1, g].reshape(n * rows, width), fresh[...], preferred_element_type=jnp.float32
                )
                .astype(jnp.bfloat16)
                .reshape(n, rows, heads)
            )
        each(n - 1, lambda k: send_sum((i + 1 + k) % n))

        @pl.when(r == 0)
        def _():
            send_sum(i)

    drain(slots.at[pl.ds(0, m - 1)], p_recv)
    mine.wait()
    total_of(slots, m, reduced, 16)

    def place(j):
        return back.at[own_half, pl.ds(pl.multiple_of((j % q) * full, full), full)]

    def block(k):
        return reduced.at[pl.ds(pl.multiple_of(k * part_rows, part_rows), part_rows)]

    def send_block(k):
        @pl.when((r == 1) | (t * q + k != i))
        def _():
            remote(block(k), place(i), b_send, b_recv, 0, t * q + k, home).start()

    each(q, send_block)

    @pl.when((r == 0) & (home == t))
    def _():
        keep = pltpu.make_async_copy(block(i % q), place(i), loc.at[0])
        keep.start()
        keep.wait()
        drain(reduced, b_recv)
        if q > 1:
            drain(reduced.at[pl.ds(0, (q - 1) * part_rows)], b_recv)
            drain(reduced.at[pl.ds(0, (q - 1) * part_rows)], b_send)

    @pl.when((r == 0) & (home != t))
    def _():
        drain(back, b_recv)
        drain(reduced, b_send)

    @pl.when(r == 0)
    def _():
        if split:
            drain(val_slots.at[pl.ds(0, n)], v_send)

    @pl.when(r == 1)
    def _():
        kept = pltpu.make_async_copy(sums.at[i], val_slots.at[n + i if split else i], loc.at[0])
        kept.start()
        drain(val_slots.at[pl.ds(0, sources - 1)], v_recv)
        kept.wait()
        total_of(val_slots, sources, vals, 16)
        each(replica_rows, finish_row)
        drain(val_slots.at[pl.ds(0, n - 1)], v_send)
        drain(reduced, b_send)

    drain(slots.at[pl.ds(0, m - 1)], p_send)

    @pl.when(active)
    def _():
        for which in range(2):
            for step in range(1, pairs):
                over(which, step).wait_send()
            for src in range(pairs):
                to_pair(which, src).wait_send()

    for role in targets:
        @pl.when(r != role)
        def _(role=role):
            drain(slabs.at[role, t], hid_send.at[role])

        @pl.when(r == role)
        def _(role=role):
            drain(slabs.at[role, t, pl.ds(0, n - 1)], hid_send.at[role])

    drain(ogs.at[pl.ds(0, n - 1)], og_send)


def fused(hid, og, master, moment1, moment2, queries, keys, k_cache, v_cache, lens, n, m):
    q = n // m
    full, heads = master.shape
    tokens = og.shape[0]
    split = full % 256 == 0
    width = full // 2 if split else full
    dma = pltpu.SemaphoreType.DMA
    anywhere = pl.BlockSpec(memory_space=pltpu.HBM)
    asked = (lens.shape[0], heads // HD, STEPS * (QH // KVH), HD)
    half = pltpu.VMEM((width, heads), jnp.float32)
    block = pltpu.VMEM((m, q * (tokens // 2), full), jnp.bfloat16)
    return pl.pallas_call(
        functools.partial(fused_kernel, n, m, split),
        out_shape=(
            jax.ShapeDtypeStruct((tokens, q * full), jnp.bfloat16),
            jax.ShapeDtypeStruct(asked, jnp.bfloat16),
        ),
        in_specs=[anywhere] * 9 + [pl.BlockSpec(memory_space=pltpu.SMEM)],
        out_specs=(anywhere, pl.BlockSpec(memory_space=pltpu.VMEM)),
        scratch_shapes=[
            pltpu.VMEM((2, m, n, tokens // m, width), jnp.bfloat16),
            pltpu.VMEM((n, tokens, heads), jnp.bfloat16),
            pltpu.VMEM((full, heads), jnp.float32),
            half,
            half,
            pltpu.VMEM((width, heads), jnp.bfloat16),
            pltpu.VMEM((n, tokens, heads), jnp.bfloat16),
            block,
            block,
            pltpu.VMEM((q * (tokens // 2), full), jnp.bfloat16),
            pltpu.VMEM((n * (2 if split else 1), tokens, heads), jnp.bfloat16),
            dma, dma, dma((2,)), dma((2,)), dma((5,)),
            dma((2, m // 2)), dma((2, m // 2)), dma((2, m // 2)), dma((2, m // 2)),
            dma, dma, dma, dma, dma, dma,
            pltpu.VMEM((tokens, heads), jnp.bfloat16),
            pltpu.VMEM(queries.shape, queries.dtype),
            pltpu.VMEM(asked, jnp.float32),
            pltpu.VMEM(keys.shape, keys.dtype),
            pltpu.VMEM(k_cache.shape, k_cache.dtype),
            pltpu.VMEM(v_cache.shape, v_cache.dtype),
            pltpu.VMEM(asked, jnp.float32),
            pltpu.VMEM(asked[:3] + (tokens,), jnp.bfloat16),
            dma((4,)),
        ],
        compiler_params=pltpu.CompilerParams(
            collective_id=0, has_side_effects=True, vmem_limit_bytes=60 * 2**20
        ),
    )(hid, og, master, moment1, moment2, queries, keys, k_cache, v_cache, lens)


def local(
    hidden, out_grad, master, moment1, moment2, queries, new_keys, k_cache, v_cache, cache_len
):
    is_learner = lax.axis_index("role") == 0
    n, m = lax.axis_size("dp"), lax.axis_size("tp")
    replica_rows = cache_len.shape[0]
    heads_here = out_grad.shape[1] // HD
    share = QH // KVH
    learner_rows, attended = fused(
        hidden[0],
        out_grad,
        master,
        moment1,
        moment2,
        queries,
        new_keys.reshape(STEPS * replica_rows, heads_here * HD),
        k_cache,
        v_cache,
        cache_len,
        n,
        m,
    )
    decoded = attended.reshape(replica_rows, heads_here, STEPS, share, HD).transpose(2, 0, 1, 3, 4)
    result = jnp.where(is_learner, learner_rows, decoded.reshape(learner_rows.shape))
    return result[None]


def solution(mesh):
    return jax.shard_map(
        local,
        mesh=mesh,
        in_specs=(
            P("role", "dp", None),
            P("dp", "tp"),
            P("dp", "tp"),
            P("dp", "tp"),
            P("dp", "tp"),
            P(None, "dp", "tp"),
            P(None, "dp", "tp"),
            P("dp", None, "tp"),
            P("dp", None, "tp"),
            P("dp"),
        ),
        out_specs=P("role", "dp", "tp"),
        check_vma=False,
    )
```

```python
import functools

import jax
import jax.numpy as jnp
from jax import lax
from jax.experimental import pallas as pl
from jax.experimental.pallas import tpu as pltpu
from jax.sharding import PartitionSpec as P

D = 8192
KVH = 8
QH = 64
HD = 128
STEPS = 8


beta_one = 0.9
beta_two = 0.95
adam_eps = 1e-08
bias_one = 1.0 - 0.9**10
bias_two = 1.0 - 0.95**10
neg_fill = -1e30


def adam_fresh(master, moment1, moment2, gradient):
    step_size = 2.0 * D ** (-0.5)
    first = beta_one * moment1 + (1.0 - beta_one) * gradient
    second = beta_two * moment2 + (1.0 - beta_two) * gradient * gradient
    change = first / bias_one / (jnp.sqrt(second / bias_two) + adam_eps)
    return (master - step_size * change).astype(jnp.bfloat16)


MESH = pl.DeviceIdType.MESH


def position():
    return lax.axis_index("role"), lax.axis_index("dp"), lax.axis_index("tp")


def signal(semaphore, role, row, col):
    pl.semaphore_signal(semaphore, inc=1, device_id=(role, row, col), device_id_type=MESH)


def remote(src, dst, send, recv, role, row, col):
    return pltpu.make_async_remote_copy(
        src_ref=src,
        dst_ref=dst,
        send_sem=send,
        recv_sem=recv,
        device_id=(role, row, col),
        device_id_type=MESH,
    )


def drain(ref, semaphore):
    pltpu.make_async_copy(ref, ref, semaphore).wait()


def each(count, body):
    def step(k, carry):
        body(k)
        return carry

    lax.fori_loop(0, count, step, 0)


def total_of(slots, count, out, tile):
    def chunk(k):
        at = pl.ds(pl.multiple_of(k * tile, tile), tile)
        total = slots[0, at, :].astype(jnp.float32)
        for s in range(1, count):
            total = total + slots[s, at, :].astype(jnp.float32)
        out[at, :] = total.astype(out.dtype)

    each(out.shape[0] // tile, chunk)


def fused_kernel(
    n, m, split, hid, og, master, moment1, moment2, queries, keys, k_cache, v_cache, lens, back, att,
    slabs, ogs, master_v, moment1_v, moment2_v, fresh, sums, parts, slots, reduced, val_slots,
    og_send, og_recv, hid_send, hid_recv, loc, x_send, x_recv, c_send, c_recv,
    p_send, p_recv, b_send, b_recv, v_send, v_recv,
    vals, queries_v, asked_v, keys_v, k_v, v_v, cache_out, fresh_wts, placed_out, placed_wts, att_sem,
):
    r, i, t = position()
    q = n // m
    rows, width = slabs.shape[3], slabs.shape[4]
    full = master.shape[0]
    heads = og.shape[1]
    home = i // q
    pairs = m // 2
    px, core = t // 2, t % 2
    sources = val_slots.shape[0]
    active = (r == 1) | split

    loads = [pltpu.make_async_copy(master, master_v, loc.at[2])]
    first = pl.multiple_of((r * width) if split else 0, width)
    for k, (src, dst) in enumerate(((moment1, moment1_v), (moment2, moment2_v))):
        loads.append(pltpu.make_async_copy(src.at[pl.ds(first, width)], dst, loc.at[3 + k]))
    for load in loads:
        load.start()

    att_loads = [
        pltpu.make_async_copy(src, dst, att_sem.at[k])
        for k, (src, dst) in enumerate(
            ((queries, queries_v), (keys, keys_v), (k_cache, k_v), (v_cache, v_v))
        )
    ]

    @pl.when(r == 1)
    def _():
        for load in att_loads:
            load.start()

    barrier = pltpu.get_barrier_semaphore()

    def greet(k):
        @pl.when(k != r * n + i)
        def _():
            signal(barrier, k // n, k % n, t)

    def greet_tp(k):
        signal(barrier, r, i, (t + 1 + k) % m)

    def greet_far(k):
        @pl.when(t * q + k != i)
        def _():
            signal(barrier, 0, t * q + k, home)

        signal(barrier, 1, t * q + k, home)

    each(2 * n, greet)
    each(m - 1, greet_tp)

    @pl.when(r == 0)
    def _():
        each(q, greet_far)
        pl.semaphore_wait(barrier, 2 * n - 1 + m - 1 + q - jnp.where(home == t, 1, 0))

    @pl.when(r == 1)
    def _():
        pl.semaphore_wait(barrier, 2 * n - 1 + m - 1 + q)

    def piece(role, j):
        start = j * full + (role * width if split else 0)
        return hid.at[pl.ds(pl.multiple_of(t * rows, rows), rows), pl.ds(pl.multiple_of(start, width), width)]

    def send_og(k):
        j = (i + k) % n
        remote(og, ogs.at[i], og_send, og_recv, r, j, t).start()

    def send_hid(role, j):
        remote(piece(role, j), slabs.at[r, t, i], hid_send.at[role], hid_recv.at[r], role, j, t).start()

    each(n - 1, lambda k: send_og(k + 1))
    targets = (0, 1) if split else (1,)
    for role in targets:
        each(n - 1, lambda k, role=role: send_hid(role, (i + k + 1) % n))

        @pl.when(r != role)
        def _(role=role):
            send_hid(role, i)

    og_local = pltpu.make_async_copy(og, ogs.at[i], loc.at[0])
    og_local.start()

    replica_rows, kv_heads, asked = asked_v.shape[:3]
    share = asked // STEPS
    half_rows = replica_rows // 2

    def attend_row(row):
        for k in range(kv_heads):
            at = slice(k * HD, (k + 1) * HD)
            cache_score, fresh_score = [
                lax.dot_general(
                    asked_v[row, k].astype(jnp.bfloat16), known, (((1,), (1,)), ((), ())), preferred_element_type=jnp.float32
                )
                * HD ** (-0.5)
                for known in (k_v[row, :, at], keys_v[:, at])
            ]
            place = lax.broadcasted_iota(jnp.int32, cache_score.shape, 1)
            cache_score = jnp.where(place < lens[row], cache_score, neg_fill)
            token = lax.broadcasted_iota(jnp.int32, fresh_score.shape, 1)
            step = lax.broadcasted_iota(jnp.int32, fresh_score.shape, 0) // share
            seen = (token % replica_rows == row) & (token // replica_rows <= step)
            fresh_score = jnp.where(seen, fresh_score, neg_fill)
            top = jnp.maximum(
                jnp.max(cache_score, axis=-1, keepdims=True), jnp.max(fresh_score, axis=-1, keepdims=True)
            )
            cache_exp = jnp.exp(cache_score - top)
            fresh_exp = jnp.exp(fresh_score - top)
            total = jnp.sum(cache_exp, axis=-1, keepdims=True) + jnp.sum(fresh_exp, axis=-1, keepdims=True)
            cache_wts = (cache_exp / total).astype(jnp.bfloat16)
            fresh_wts[row, k] = fresh_exp / total
            cache_out[row, k] = jnp.dot(cache_wts, v_v[row, :, at], preferred_element_type=jnp.float32)

    def place_rows():
        for s in range(STEPS):
            at = slice(s * replica_rows, (s + 1) * replica_rows)
            for k in range(kv_heads):
                for h in range(share):
                    head = k * share + h
                    placed_out[at, head * HD : (head + 1) * HD] = cache_out[:, k, s * share + h, :]
                    placed_wts[head, at, :] = fresh_wts[:, k, s * share + h, :].astype(jnp.bfloat16)

    def finish():
        for k in range(kv_heads):
            new_values = vals[:, k * HD : (k + 1) * HD]
            for head in range(k * share, (k + 1) * share):
                at = slice(head * HD, (head + 1) * HD)
                new = jnp.dot(placed_wts[head], new_values, preferred_element_type=jnp.float32)
                att[:, at] = (placed_out[:, at] + new).astype(att.dtype)

    drain(ogs.at[pl.ds(0, n - 1)], og_recv)
    og_local.wait()
    for load in loads:
        load.wait()

    chunk = min(512, full)
    part_rows = og.shape[0] // 2
    block_rows = q * part_rows
    own_half = pl.ds(pl.multiple_of(r * part_rows, part_rows), part_rows)

    def fill_part(g):
        tokens = ogs[pl.ds(g * q, q), own_half, :].reshape(block_rows, heads)

        def columns(k):
            at = pl.ds(pl.multiple_of(k * chunk, chunk), chunk)
            parts[g, :, at] = lax.dot_general(
                tokens,
                master_v[at, :].astype(jnp.bfloat16),
                (((1,), (1,)), ((), ())),
                preferred_element_type=jnp.float32,
            ).astype(jnp.bfloat16)

        each(full // chunk, columns)

    mine = pltpu.make_async_copy(parts.at[t], slots.at[t], loc.at[0])

    def send_part(k):
        g = (t + 1 + k) % m
        fill_part(g)
        remote(parts.at[g], slots.at[t], p_send, p_recv, r, i, g).start()

    each(m - 1, send_part)
    fill_part(t)
    mine.start()

    @pl.when(r == 1)
    def _():
        for load in att_loads:
            load.wait()

        for s in range(STEPS):
            for k in range(kv_heads):
                for h in range(share):
                    at = (k * share + h) * HD
                    asked_v[:, k, s * share + h, :] = queries_v[s, :, at : at + HD].astype(jnp.float32)

        each(half_rows, attend_row)

    def to_pair(which, src):
        return remote(
            slabs.at[which, src * 2 + core],
            slabs.at[which, src * 2 + core],
            c_send.at[which, src],
            c_recv.at[which, src],
            r, i, t + 1 - 2 * core,
        )

    def from_pair(which, src):
        drain(slabs.at[which, src * 2 + 1 - core], c_recv.at[which, src])

    def over(which, step):
        dst = (px + step) % pairs
        return remote(
            slabs.at[which, t],
            slabs.at[which, t],
            x_send.at[which, step],
            x_recv.at[which, px],
            r, i, dst * 2 + core,
        )

    @pl.when(active)
    def _():
        own = pltpu.make_async_copy(piece(r, i), slabs.at[r, t, i], loc.at[1])
        own.start()
        for which in range(2):
            @pl.when(r != which)
            def _(which=which):
                drain(slabs.at[which, t], hid_recv.at[which])

            @pl.when(r == which)
            def _(which=which):
                drain(slabs.at[which, t, pl.ds(0, n - 1)], hid_recv.at[which])
                own.wait()

            for step in range(1, pairs):
                over(which, step).start()
            to_pair(which, px).start()

    @pl.when(r == 1)
    def _():
        each(replica_rows - half_rows, lambda k: attend_row(half_rows + k))
        place_rows()

    def send_sum(j):
        slot = r * n + i if split else i
        remote(sums.at[j], val_slots.at[slot], v_send, v_recv, 1, j, t).start()

    @pl.when(active)
    def _():
        for which in range(2):
            for step in range(1, pairs):
                src = (px + step) % pairs
                drain(slabs.at[which, src * 2 + core], x_recv.at[which, src])
                to_pair(which, src).start()
        for src in range(pairs):
            from_pair(0, src)

        tile = min(256, width)

        def update(k):
            at = pl.ds(pl.multiple_of(k * tile, tile), tile)
            gradient = jnp.zeros((tile, heads), jnp.float32)
            for g in range(m):
                gradient = gradient + lax.dot_general(
                    slabs[0, g, :, :, at].reshape(n * rows, tile),
                    ogs[:, g * rows : (g + 1) * rows, :].reshape(n * rows, heads),
                    (((0,), (0,)), ((), ())),
                    preferred_element_type=jnp.float32,
                )
            held = pl.ds(pl.multiple_of(first + k * tile, tile), tile)
            fresh[at, :] = adam_fresh(master_v[held, :], moment1_v[at, :], moment2_v[at, :], gradient)

        each(width // tile, update)
        for src in range(pairs):
            from_pair(1, src)
        for g in range(m):
            sums[:, g * rows : (g + 1) * rows, :] = (
                jnp.dot(
                    slabs[1, g].reshape(n * rows, width), fresh[...], preferred_element_type=jnp.float32
                )
                .astype(jnp.bfloat16)
                .reshape(n, rows, heads)
            )
        each(n - 1, lambda k: send_sum((i + 1 + k) % n))

        @pl.when(r == 0)
        def _():
            send_sum(i)

    drain(slots.at[pl.ds(0, m - 1)], p_recv)
    mine.wait()
    total_of(slots, m, reduced, 16)

    def place(j):
        return back.at[own_half, pl.ds(pl.multiple_of((j % q) * full, full), full)]

    def block(k):
        return reduced.at[pl.ds(pl.multiple_of(k * part_rows, part_rows), part_rows)]

    def send_block(k):
        @pl.when((r == 1) | (t * q + k != i))
        def _():
            remote(block(k), place(i), b_send, b_recv, 0, t * q + k, home).start()

    each(q, send_block)

    @pl.when((r == 0) & (home == t))
    def _():
        keep = pltpu.make_async_copy(block(i % q), place(i), loc.at[0])
        keep.start()
        keep.wait()
        drain(reduced, b_recv)
        if q > 1:
            drain(reduced.at[pl.ds(0, (q - 1) * part_rows)], b_recv)
            drain(reduced.at[pl.ds(0, (q - 1) * part_rows)], b_send)

    @pl.when((r == 0) & (home != t))
    def _():
        drain(back, b_recv)
        drain(reduced, b_send)

    @pl.when(r == 0)
    def _():
        if split:
            drain(val_slots.at[pl.ds(0, n)], v_send)

    @pl.when(r == 1)
    def _():
        kept = pltpu.make_async_copy(sums.at[i], val_slots.at[n + i if split else i], loc.at[0])
        kept.start()
        drain(val_slots.at[pl.ds(0, sources - 1)], v_recv)
        kept.wait()
        total_of(val_slots, sources, vals, 16)
        finish()
        drain(val_slots.at[pl.ds(0, n - 1)], v_send)
        drain(reduced, b_send)

    drain(slots.at[pl.ds(0, m - 1)], p_send)

    @pl.when(active)
    def _():
        for which in range(2):
            for step in range(1, pairs):
                over(which, step).wait_send()
            for src in range(pairs):
                to_pair(which, src).wait_send()

    for role in targets:
        @pl.when(r != role)
        def _(role=role):
            drain(slabs.at[role, t], hid_send.at[role])

        @pl.when(r == role)
        def _(role=role):
            drain(slabs.at[role, t, pl.ds(0, n - 1)], hid_send.at[role])

    drain(ogs.at[pl.ds(0, n - 1)], og_send)


def fused(hid, og, master, moment1, moment2, queries, keys, k_cache, v_cache, lens, n, m):
    q = n // m
    full, heads = master.shape
    tokens = og.shape[0]
    split = full % 256 == 0
    width = full // 2 if split else full
    dma = pltpu.SemaphoreType.DMA
    anywhere = pl.BlockSpec(memory_space=pltpu.HBM)
    asked = (lens.shape[0], heads // HD, STEPS * (QH // KVH), HD)
    half = pltpu.VMEM((width, heads), jnp.float32)
    block = pltpu.VMEM((m, q * (tokens // 2), full), jnp.bfloat16)
    return pl.pallas_call(
        functools.partial(fused_kernel, n, m, split),
        out_shape=(
            jax.ShapeDtypeStruct((tokens, q * full), jnp.bfloat16),
            jax.ShapeDtypeStruct((tokens, queries.shape[2]), jnp.bfloat16),
        ),
        in_specs=[anywhere] * 9 + [pl.BlockSpec(memory_space=pltpu.SMEM)],
        out_specs=(anywhere, pl.BlockSpec(memory_space=pltpu.VMEM)),
        scratch_shapes=[
            pltpu.VMEM((2, m, n, tokens // m, width), jnp.bfloat16),
            pltpu.VMEM((n, tokens, heads), jnp.bfloat16),
            pltpu.VMEM((full, heads), jnp.float32),
            half,
            half,
            pltpu.VMEM((width, heads), jnp.bfloat16),
            pltpu.VMEM((n, tokens, heads), jnp.bfloat16),
            block,
            block,
            pltpu.VMEM((q * (tokens // 2), full), jnp.bfloat16),
            pltpu.VMEM((n * (2 if split else 1), tokens, heads), jnp.bfloat16),
            dma, dma, dma((2,)), dma((2,)), dma((5,)),
            dma((2, m // 2)), dma((2, m // 2)), dma((2, m // 2)), dma((2, m // 2)),
            dma, dma, dma, dma, dma, dma,
            pltpu.VMEM((tokens, heads), jnp.bfloat16),
            pltpu.VMEM(queries.shape, queries.dtype),
            pltpu.VMEM(asked, jnp.float32),
            pltpu.VMEM(keys.shape, keys.dtype),
            pltpu.VMEM(k_cache.shape, k_cache.dtype),
            pltpu.VMEM(v_cache.shape, v_cache.dtype),
            pltpu.VMEM(asked, jnp.float32),
            pltpu.VMEM(asked[:3] + (tokens,), jnp.float32),
            pltpu.VMEM((tokens, queries.shape[2]), jnp.float32),
            pltpu.VMEM((queries.shape[2] // HD, tokens, tokens), jnp.bfloat16),
            dma((4,)),
        ],
        compiler_params=pltpu.CompilerParams(
            collective_id=0, has_side_effects=True, vmem_limit_bytes=60 * 2**20
        ),
    )(hid, og, master, moment1, moment2, queries, keys, k_cache, v_cache, lens)


def local(
    hidden, out_grad, master, moment1, moment2, queries, new_keys, k_cache, v_cache, cache_len
):
    is_learner = lax.axis_index("role") == 0
    n, m = lax.axis_size("dp"), lax.axis_size("tp")
    replica_rows = cache_len.shape[0]
    heads_here = out_grad.shape[1] // HD
    learner_rows, attended = fused(
        hidden[0],
        out_grad,
        master,
        moment1,
        moment2,
        queries,
        new_keys.reshape(STEPS * replica_rows, heads_here * HD),
        k_cache,
        v_cache,
        cache_len,
        n,
        m,
    )
    result = jnp.where(is_learner, learner_rows, attended)
    return result[None]


def solution(mesh):
    return jax.shard_map(
        local,
        mesh=mesh,
        in_specs=(
            P("role", "dp", None),
            P("dp", "tp"),
            P("dp", "tp"),
            P("dp", "tp"),
            P("dp", "tp"),
            P(None, "dp", "tp"),
            P(None, "dp", "tp"),
            P("dp", None, "tp"),
            P("dp", None, "tp"),
            P("dp"),
        ),
        out_specs=P("role", "dp", "tp"),
        check_vma=False,
    )
```
